128 devices in a mesh: replica: 4 (over y_hi, core), shard: 32 (over z, x, y_lo).
Axes of the slice: x: 4, y: 4 (y_hi: 2, y_lo: 2; y = y_hi * 2 + y_lo), z: 4, core: 2. Of those that a mesh axis runs over, the one named last changes fastest.
Arguments:
- tokens: bfloat16 [81920, 8192], P(('replica', 'shard')), may hold values from -6 to 6
- cotangent: bfloat16 [81920, 512], P(('replica', 'shard')), may hold values from -6 to 6
- inner_weight: float32 [4, 8192, 512], P('replica', 'shard'), may hold values from -6 to 6
- first_moment: float32 [4, 8192, 512], P('replica', 'shard'), may hold values from -6 to 6
- second_moment: float32 [4, 8192, 512], P('replica', 'shard'), may hold values from 0.05 to 5
- outer_params: float32 [8192, 128], P(('shard', 'replica')), may hold values from -6 to 6
- outer_momentum: float32 [8192, 128], P(('shard', 'replica')), may hold values from -4 to 4
- fragment: int32 [1], replicated, may hold values from 0 to 3
Outputs:
- keys: bfloat16 [81920, 512], P(('replica', 'shard'))
- input_grad: bfloat16 [81920, 8192], P(('replica', 'shard'))
- inner_next: float32 [4, 8192, 512], P('replica', 'shard')
- first_next: float32 [4, 8192, 512], P('replica', 'shard')
- second_next: float32 [4, 8192, 512], P('replica', 'shard')
- outer_next: float32 [8192, 128], P(('shard', 'replica'))
- momentum_next: float32 [8192, 128], P(('shard', 'replica'))
The draws below stay inside these ranges and needn't reach their ends.
All inputs are finite; a program needn't handle non-finite values.
Results may differ from the reference program's by a relative error of at most 0.005.
Values may be sent and summed in bfloat16 or wider, within the bound.
A program may use at most 192 MiB of HBM per device.

```python
import math
import jax
import jax.numpy as jnp
from jax import lax

D = 8192
NFRAG = 4
TOK_DEV = 640
KW = 512
FRAGW = 128
TOKENS = 81920
REPLICAS = 4
N_REPLICA = 4
N_SHARD = 32


def block_levels(own_key, dims, cuts, smallest, high):
    level, own = 1.0, jax.random.fold_in(own_key, 6)
    for dim, parts in cuts:
        heights = jnp.exp(jax.random.uniform(jax.random.fold_in(own, dim), (parts,), jnp.float32, smallest / len(cuts), high / len(cuts)))
        level = level * jnp.repeat(heights, dims[dim] // parts).reshape([-1 if axis == dim else 1 for axis in range(len(dims))])
    return level


def centred(key, shape, width, most, shards=(), kind=jnp.bfloat16):
    factor_of = block_levels(key, shape, shards, -0.22, 0.18) if shards else 1.0
    result = jax.random.normal(key, shape, jnp.float32) * width * factor_of
    return jnp.minimum(jnp.maximum(result, -most), most).astype(kind)


def setup_inputs(seed: int = 0) -> dict:
    splits = jax.random.split(jax.random.key(seed), 9)
    return {
        "tokens": centred(splits[0], (TOKENS, D), 1.0, 6.0, ((0, 128),)),
        "cotangent": centred(splits[1], (TOKENS, KW), 1.0, 6.0, ((0, 128),)),
        "inner_weight": centred(splits[2], (REPLICAS, D, KW), 1.0, 6.0, ((0, 4), (1, 32)), jnp.float32),
        "first_moment": centred(splits[3], (REPLICAS, D, KW), 1.0, 6.0, ((0, 4), (1, 32)), jnp.float32),
        "second_moment": jnp.clip(jnp.exp(math.log(5.0) - 4.6051702 * jax.random.uniform(splits[4], (REPLICAS, D, KW), jnp.float32) ** block_levels(splits[4], (REPLICAS, D, KW), ((0, 4), (1, 32)), -0.2, 0.2)), 0.05, 5.0),
        "outer_params": centred(splits[5], (D, FRAGW), 1.0, 6.0, ((0, 128),), jnp.float32),
        "outer_momentum": centred(splits[6], (D, FRAGW), 0.5, 4.0, ((0, 128),), jnp.float32),
        "fragment": jax.random.randint(splits[7], (1,), 0, NFRAG).astype(jnp.int32),
    }


beta_first = 0.9
beta_second = 0.95
adam_rate = 0.05
decay_rate = 0.1
adam_eps = 1e-08
correction_first = 0.9999734386011124
correction_second = 0.994079470779666
outer_rate = 0.7
outer_beta = 0.9
mixing_weight = 0.5

def adam_update(weight, grad, first_moment, second_moment):
    first_next = beta_first * first_moment + (1.0 - beta_first) * grad
    second_next = beta_second * second_moment + (1.0 - beta_second) * grad * grad
    step_size = first_next / correction_first / (jnp.sqrt(second_next / correction_second) + adam_eps)
    weight_next = weight - adam_rate * (step_size + decay_rate * weight)
    return (weight_next, first_next, second_next)

def nesterov(outer_params, outer_momentum, mean_inner):
    pseudo = outer_params - mean_inner
    momentum_next = outer_beta * outer_momentum + pseudo
    params_next = outer_params - outer_rate * (pseudo + outer_beta * momentum_next)
    return (params_next, momentum_next)

def reference(tokens, cotangent, inner_weight, first_moment, second_moment, outer_params, outer_momentum, fragment):
    replica_tokens = TOK_DEV * N_SHARD
    scale = D ** (-0.5)
    grad_scale = replica_tokens ** (-0.5)
    key_parts = []
    input_parts = []
    weight_parts = []
    first_parts = []
    second_parts = []
    for replica in range(N_REPLICA):
        token_rows = tokens[replica * replica_tokens:(replica + 1) * replica_tokens]
        cot_rows = cotangent[replica * replica_tokens:(replica + 1) * replica_tokens]
        weight_low = inner_weight[replica].astype(jnp.bfloat16)
        key_parts.append((jnp.dot(token_rows, weight_low, preferred_element_type=jnp.float32) * scale).astype(jnp.bfloat16))
        input_parts.append((jnp.dot(cot_rows, weight_low.T, preferred_element_type=jnp.float32) * scale).astype(jnp.bfloat16))
        grad = jnp.dot(token_rows.T, cot_rows, preferred_element_type=jnp.float32) * grad_scale
        weight_next, first_next, second_next = adam_update(inner_weight[replica], grad, first_moment[replica], second_moment[replica])
        weight_parts.append(weight_next)
        first_parts.append(first_next)
        second_parts.append(second_next)
    weight_all = jnp.stack(weight_parts)
    first_col = (fragment[0] * FRAGW).astype(jnp.int32)
    blocks = lax.dynamic_slice_in_dim(weight_all, first_col, FRAGW, 2)
    mean_inner = lax.optimization_barrier(jnp.sum(blocks, axis=0)) / N_REPLICA
    params_next, momentum_next = nesterov(outer_params, outer_momentum, mean_inner)
    mixed = mixing_weight * blocks + (1.0 - mixing_weight) * params_next[None]
    inner_next = lax.dynamic_update_slice_in_dim(weight_all, mixed, first_col, 2)
    return (jnp.concatenate(key_parts, 0), jnp.concatenate(input_parts, 0), inner_next, jnp.stack(first_parts), jnp.stack(second_parts), params_next, momentum_next)
```

```python
import functools

import jax
import jax.numpy as jnp
from jax import lax
from jax.experimental import pallas as pl
from jax.experimental.pallas import tpu as pltpu
from jax.sharding import PartitionSpec as P

MESH = pl.DeviceIdType.MESH
BF16 = jnp.bfloat16
F32 = jnp.float32

beta_first = 0.9
beta_second = 0.95
adam_rate = 0.05
decay_rate = 0.1
adam_eps = 1e-08
correction_first = 0.9999734386011124
correction_second = 0.994079470779666
outer_rate = 0.7
outer_beta = 0.9
mixing_weight = 0.5

D, KW, FRAGW, TOK, ROWS = 8192, 512, 128, 640, 256
NSHARD, NREP = 32, 4
SCALE = D ** (-0.5)
GRAD_SCALE = (TOK * NSHARD) ** (-0.5)
NSTREAM = 4
PART = ROWS // NSTREAM

LINKS = ("x+", "x-", "z+", "z-", "y")
BACK = {"x+": "x-", "x-": "x+", "z+": "z-", "z-": "z+", "y": "y"}
ROOT = (0, 0, 0)
NODES = [(x, y, z) for z in (2, 1, 3, 0) for x in (2, 1, 3, 0) for y in (1, 0)]
TREES = (("x", 1), ("z", 1), ("x", -1), ("z", -1))

SEND_US = 1.42
HOP_US = 2.0
GRAD_US = 0.45
KEYS_US = 0.45
ADD_US = 0.25
ISSUE_US = 0.05
DEPTH = 4


def tree_parent(tree, node):
    first, sign = tree
    x, y, z = node
    a, b = (x, z) if first == "x" else (z, x)
    second = "z" if first == "x" else "x"

    def back(v):
        if sign > 0:
            return {1: (0, "+"), 2: (1, "+"), 3: (0, "-")}[v]
        return {3: (0, "-"), 2: (3, "-"), 1: (0, "+")}[v]

    if b == 2 and y == 1 and a in (0, 2):
        a, y, b, link = a, 0, b, "y"
    elif b:
        b, way = back(b)
        link = second + way
    elif y:
        y, link = 0, "y"
    else:
        a, way = back(a)
        link = first + way
    return ((a, y, b) if first == "x" else (b, y, a)), link


def make_trees():
    parent, children = {}, {}
    for s, tree in enumerate(TREES):
        for node in NODES:
            children.setdefault((s, node), [])
        for node in NODES:
            if node != ROOT:
                up, link = tree_parent(tree, node)
                parent[s, node] = (up, link)
                children[s, up].append((node, link))
    return parent, children


PARENT, CHILDREN = make_trees()
EDGES = {key: i for i, key in enumerate(sorted(PARENT))}


def plan_links():
    def height(key):
        return 1 + max([height((key[0], c)) for c, _ in CHILDREN[key]], default=0)

    def weight(key):
        return 1 + sum(weight((key[0], c)) for c, _ in CHILDREN[key])

    def depth(key):
        return 0 if key[1] == ROOT else 1 + depth((key[0], PARENT[key][0]))

    grads_done = NSHARD * GRAD_US + 3.0
    waiting = {key: len(v) for key, v in CHILDREN.items()}
    latest = {key: 0.0 for key in CHILDREN}
    ready = {link: [] for link in LINKS}
    free = {link: 0.0 for link in LINKS}
    for s in range(NSTREAM):
        for node, link in CHILDREN[s, ROOT]:
            ready[link].append((0.0, "gather", s, node))
    for key in PARENT:
        if not waiting[key]:
            ready[BACK[PARENT[key][1]]].append((grads_done, "reduce") + key)
    sends, arrival, roots = [], {}, {}
    while any(ready.values()):
        at, link = min((max(free[k], min(r[0] for r in v)), k) for k, v in ready.items() if v)
        open_now = [r for r in ready[link] if r[0] <= at + 1e-9]

        def rank(r):
            key = r[2:]
            if r[1] == "reduce":
                return (1, depth(key), 0, -EDGES[key])
            return (0, height(key), weight(key), -EDGES[key])

        pick = max(open_now, key=rank)
        ready[link].remove(pick)
        _, kind, s, node = pick
        free[link] = at + SEND_US
        there = at + SEND_US + HOP_US
        sends.append((at, link, kind, s, node))
        arrival[kind, s, node] = there
        if kind == "gather":
            for child, way in CHILDREN[s, node]:
                ready[way].append((there, "gather", s, child))
        else:
            up = (s, PARENT[s, node][0])
            waiting[up] -= 1
            latest[up] = max(latest[up], there)
            if not waiting[up]:
                if up[1] == ROOT:
                    roots[s] = latest[up]
                else:
                    ready[BACK[PARENT[up][1]]].append((max(latest[up] + ADD_US, grads_done), "reduce") + up)
    return sends, arrival, max(roots.values())


def make_program():
    sends, arrival, roots_at = plan_links()
    full_at = {n: max(arrival["gather", s, n] for s in range(NSTREAM)) for n in NODES if n != ROOT}
    full_at[ROOT] = 0.0
    keys_left = sorted(NODES, key=lambda n: full_at[n])
    tail = [(roots_at, "update"), (roots_at + 6.0, "outer"), (roots_at + 12.0, "spread")]
    events = sorted([(t, 1, ("send",) + tuple(r)) for t, *r in sends] + [(t, 0, (n,)) for t, n in tail], key=lambda e: e[:2])
    program, now, grads = [], 0.0, 0
    for at, _, op in events:
        while True:
            if grads < NSHARD and (now + 0.5 * GRAD_US < at or op[0] != "send" or op[2] == "reduce"):
                program.append(("grad", grads))
                grads += 1
                now += GRAD_US
            elif grads == NSHARD and keys_left and full_at[keys_left[0]] < now and now + 0.5 * KEYS_US < at:
                program.append(("keys", keys_left.pop(0)))
                now += KEYS_US
            else:
                break
        now = max(now, at) + (ADD_US if op[0] == "send" and op[2] == "reduce" else ISSUE_US)
        program.append(op)
    program += [("keys", n) for n in keys_left]
    return program


def adam(weight, grad, first, second):
    first_next = beta_first * first + (1.0 - beta_first) * grad
    second_next = beta_second * second + (1.0 - beta_second) * grad * grad
    step = first_next / correction_first / (jnp.sqrt(second_next / correction_second) + adam_eps)
    return weight - adam_rate * (step + decay_rate * weight), first_next, second_next


def select_block(fragment, array):
    block = array[:, :FRAGW]
    for f in range(1, KW // FRAGW):
        block = jnp.where(fragment == f, array[:, f * FRAGW : (f + 1) * FRAGW], block)
    return block


def exchange_kernel(
    fragment_ref, tokens_hbm, cot_hbm, weight_hbm, first_hbm, second_hbm, outer_hbm, mom_hbm,
    full_hbm, keys_ref, grad_ref, block_ref, outer_ref, mom_ref,
    tokens, cot, weight, first, second, outer, mom, full, sums, landed, keys_acc, inner, peers, spread,
    in_sem, full_sem, send_sem, gather_sem, reduce_sem, peer_send, peer_recv, spread_send, spread_recv,
):
    shard, rep = lax.axis_index("shard"), lax.axis_index("replica")
    my, mx, mz = shard % 2, (shard // 2) % 4, shard // 8
    core, high = rep % 2, rep // 2

    def owner(node):
        x, y, z = node
        return (((mz + 4 - z) % 4) * 4 + (mx + 4 - x) % 4) * 2 + (my + y) % 2

    def shard_at(link):
        x, y, z = mx, my, mz
        if link == "y":
            y = 1 - y
        elif link[0] == "x":
            x = (x + (1 if link[1] == "+" else 3)) % 4
        else:
            z = (z + (1 if link[1] == "+" else 3)) % 4
        return (z * 4 + x) * 2 + y

    there = {link: {"shard": shard_at(link)} for link in LINKS}
    peer = [high * 2 + 1 - core, (1 - high) * 2 + core, (1 - high) * 2 + 1 - core]

    def local(src, dst, i):
        return pltpu.make_async_copy(src, dst, in_sem.at[i])

    loads = [
        local(weight_hbm.at[0], weight, 0),
        local(cot_hbm, cot, 1),
        local(tokens_hbm, tokens, 2),
        local(first_hbm.at[0], first, 3),
        local(second_hbm.at[0], second, 4),
        local(outer_hbm, outer, 5),
        local(mom_hbm, mom, 6),
    ]
    for copy in loads:
        copy.start()
    barrier = pltpu.get_barrier_semaphore()
    for link in LINKS:
        pl.semaphore_signal(barrier, inc=1, device_id=there[link], device_id_type=MESH)
    for p in peer:
        pl.semaphore_signal(barrier, inc=1, device_id={"replica": p}, device_id_type=MESH)
    loads[0].wait()
    full[shard] = weight[...].astype(BF16)
    pl.semaphore_wait(barrier, 8)

    def part(s):
        return pl.ds(s * PART, PART)

    issued = {link: [] for link in LINKS}
    waited = set()
    full_copies = []

    def send_copy(kind, s, node, slot):
        edge = EDGES[s, node]
        up, link = PARENT[s, node]
        if kind == "gather":
            where = full.at[owner(up), part(s)]
            return pltpu.make_async_remote_copy(
                src_ref=where, dst_ref=where, send_sem=send_sem.at[LINKS.index(link), slot],
                recv_sem=gather_sem.at[edge], device_id=there[link], device_id_type=MESH,
            )
        link = BACK[link]
        return pltpu.make_async_remote_copy(
            src_ref=sums.at[owner(node), part(s)], dst_ref=landed.at[edge],
            send_sem=send_sem.at[LINKS.index(link), slot],
            recv_sem=reduce_sem.at[edge], device_id=there[link], device_id_type=MESH,
        )

    def arrived(kind, s, node):
        if (kind, s, node) in waited or node == ROOT:
            return
        waited.add((kind, s, node))
        edge = EDGES[s, node]
        if kind == "gather":
            where = full.at[owner(node), part(s)]
            pltpu.make_async_copy(where, where, gather_sem.at[edge]).wait()
        else:
            where = landed.at[edge]
            pltpu.make_async_copy(where, where, reduce_sem.at[edge]).wait()

    def summed(s, node):
        total = sums[owner(node), part(s)].astype(F32)
        for child, _ in CHILDREN[s, node]:
            arrived("reduce", s, child)
            total = total + landed[EDGES[s, child]].astype(F32)
        return total

    def send(link, kind, s, node):
        if kind == "gather":
            arrived("gather", s, PARENT[s, node][0])
        elif CHILDREN[s, node]:
            sums[owner(node), part(s)] = summed(s, node).astype(BF16)
        line = issued[link]
        if len(line) >= DEPTH:
            line[-DEPTH].wait_send()
        copy = send_copy(kind, s, node, len(line) % DEPTH)
        copy.start()
        line.append(copy)

    def grad_tile(i, carry):
        z, x, y = (2 + i // 8) % 4, (2 + (i % 8) // 2) % 4, 1 - i % 2
        which = owner((x, y, z))
        cols = pl.ds(pl.multiple_of(which * ROWS, ROWS), ROWS)
        sums[which] = lax.dot_general(
            tokens[:, cols], cot[...], (((0,), (0,)), ((), ())), preferred_element_type=F32
        ).astype(BF16)
        return carry

    def keys_tile(node, begin):
        for s in range(NSTREAM):
            arrived("gather", s, node)
        which = owner(node)
        copy = pltpu.make_async_copy(full.at[which], full_hbm.at[which], full_sem.at[NODES.index(node)])
        copy.start()
        full_copies.append(copy)
        cols = pl.ds(pl.multiple_of(which * ROWS, ROWS), ROWS)
        term = jnp.dot(tokens[:, cols], full[which], preferred_element_type=F32)
        if begin:
            keys_acc[...] = term
        else:
            keys_acc[...] += term

    mine = pl.ds(pl.multiple_of(rep * (ROWS // NREP), ROWS // NREP), ROWS // NREP)

    def update():
        for s in range(NSTREAM):
            grad_ref[part(s), :] = summed(s, ROOT) * GRAD_SCALE
        for copy in loads[3:]:
            copy.wait()
        f = fragment_ref[0]
        inner[...] = adam(
            select_block(f, weight[...]), select_block(f, grad_ref[...]),
            select_block(f, first[...]), select_block(f, second[...]),
        )[0]
        for copy in to_peers():
            copy.start()

    def to_peers():
        return [
            pltpu.make_async_remote_copy(
                src_ref=inner.at[pl.ds(pl.multiple_of(p * (ROWS // NREP), ROWS // NREP), ROWS // NREP)],
                dst_ref=peers.at[k], send_sem=peer_send.at[k], recv_sem=peer_recv.at[k],
                device_id={"replica": p}, device_id_type=MESH,
            )
            for k, p in enumerate(peer)
        ]

    def to_all():
        return [
            pltpu.make_async_remote_copy(
                src_ref=spread.at[mine], dst_ref=spread.at[mine], send_sem=spread_send.at[k],
                recv_sem=spread_recv.at[k], device_id={"replica": p}, device_id_type=MESH,
            )
            for k, p in enumerate(peer)
        ]

    def outer_step():
        total = inner[mine]
        for k, copy in enumerate(to_peers()):
            copy.wait_recv()
            total = total + peers[k]
        pseudo = outer[...] - total / NREP
        mom_next = outer_beta * mom[...] + pseudo
        outer_next = outer[...] - outer_rate * (pseudo + outer_beta * mom_next)
        outer_ref[...] = outer_next
        mom_ref[...] = mom_next
        spread[mine] = outer_next
        for copy in to_all():
            copy.start()

    def spread_step():
        for k, p in enumerate(peer):
            rows = pl.ds(pl.multiple_of(p * (ROWS // NREP), ROWS // NREP), ROWS // NREP)
            pltpu.make_async_copy(spread.at[rows], spread.at[rows], spread_recv.at[k]).wait()
        block_ref[...] = spread[...]

    program = make_program()
    at, begin = 0, True
    while at < len(program):
        op = program[at]
        if op[0] == "grad":
            if op[1] == 0:
                loads[1].wait()
                loads[2].wait()
            n = 1
            while at + n < len(program) and program[at + n][0] == "grad":
                n += 1
            lax.fori_loop(op[1], op[1] + n, grad_tile, 0)
            at += n
            continue
        if op[0] == "send":
            send(*op[1:])
        elif op[0] == "keys":
            keys_tile(op[1], begin)
            begin = False
        else:
            {"update": update, "outer": outer_step, "spread": spread_step}[op[0]]()
        at += 1

    keys_ref[...] = (keys_acc[...] * SCALE).astype(BF16)
    for line in issued.values():
        for copy in line[-DEPTH:]:
            copy.wait_send()
    for copy in to_peers() + to_all():
        copy.wait_send()
    for copy in full_copies:
        copy.wait()


def finish_kernel(
    fragment_ref, cot_ref, full_ref, weight_ref, first_ref, second_ref, grad_ref, block_ref, keys_in, outer_in, mom_in,
    input_ref, keys_ref, inner_ref, first_out, second_out, outer_ref, mom_ref,
):
    total = lax.dot_general(cot_ref[...], full_ref[...], (((1,), (1,)), ((), ())), preferred_element_type=F32)
    input_ref[...] = (total * SCALE).astype(BF16)
    keys_ref[...] = keys_in[...]
    outer_ref[...] = outer_in[...]
    mom_ref[...] = mom_in[...]
    weight_next, first_next, second_next = adam(weight_ref[0], grad_ref[...], first_ref[0], second_ref[0])
    first_out[0] = first_next
    second_out[0] = second_next
    for f in range(KW // FRAGW):
        cols = slice(f * FRAGW, (f + 1) * FRAGW)
        old = weight_next[:, cols]
        mixed = mixing_weight * old + (1.0 - mixing_weight) * block_ref[...]
        inner_ref[0, :, cols] = jnp.where(fragment_ref[0] == f, mixed, old)


def exchange(fragment, tokens, cotangent, inner_weight, first_moment, second_moment, outer_params, outer_momentum):
    anyspace = pl.BlockSpec(memory_space=pl.ANY)
    vmem = pl.BlockSpec(memory_space=pltpu.VMEM)
    edges = len(EDGES)
    return pl.pallas_call(
        exchange_kernel,
        out_shape=(
            jax.ShapeDtypeStruct((NSHARD, ROWS, KW), BF16),
            jax.ShapeDtypeStruct((TOK, KW), BF16),
            jax.ShapeDtypeStruct((ROWS, KW), F32),
            jax.ShapeDtypeStruct((ROWS, FRAGW), F32),
            jax.ShapeDtypeStruct((ROWS // NREP, FRAGW), F32),
            jax.ShapeDtypeStruct((ROWS // NREP, FRAGW), F32),
        ),
        in_specs=[pl.BlockSpec(memory_space=pltpu.SMEM)] + [anyspace] * 7,
        out_specs=(anyspace, vmem, vmem, vmem, vmem, vmem),
        scratch_shapes=[
            pltpu.VMEM((TOK, D), BF16),
            pltpu.VMEM((TOK, KW), BF16),
            pltpu.VMEM((ROWS, KW), F32),
            pltpu.VMEM((ROWS, KW), F32),
            pltpu.VMEM((ROWS, KW), F32),
            pltpu.VMEM((ROWS // NREP, FRAGW), F32),
            pltpu.VMEM((ROWS // NREP, FRAGW), F32),
            pltpu.VMEM((NSHARD, ROWS, KW), BF16),
            pltpu.VMEM((NSHARD, ROWS, KW), BF16),
            pltpu.VMEM((edges, PART, KW), BF16),
            pltpu.VMEM((TOK, KW), F32),
            pltpu.VMEM((ROWS, FRAGW), F32),
            pltpu.VMEM((NREP - 1, ROWS // NREP, FRAGW), F32),
            pltpu.VMEM((ROWS, FRAGW), F32),
            pltpu.SemaphoreType.DMA((7,)),
            pltpu.SemaphoreType.DMA((NSHARD,)),
            pltpu.SemaphoreType.DMA((len(LINKS), DEPTH)),
            pltpu.SemaphoreType.DMA((edges,)),
            pltpu.SemaphoreType.DMA((edges,)),
            pltpu.SemaphoreType.DMA((NREP - 1,)),
            pltpu.SemaphoreType.DMA((NREP - 1,)),
            pltpu.SemaphoreType.DMA((NREP - 1,)),
            pltpu.SemaphoreType.DMA((NREP - 1,)),
        ],
        compiler_params=pltpu.CompilerParams(
            collective_id=0, has_side_effects=True, vmem_limit_bytes=56 * 2**20
        ),
        cost_estimate=pl.CostEstimate(
            flops=4 * TOK * D * KW, bytes_accessed=30 * 2**20, transcendentals=0
        ),
        name="exchange",
    )(fragment, tokens, cotangent, inner_weight, first_moment, second_moment, outer_params, outer_momentum)


def finish(fragment, cotangent, full, inner_weight, first_moment, second_moment, grad, block, keys, outer, mom):
    steps = 8
    rows, toks, own, cols = ROWS // steps, TOK // steps, ROWS // NREP // steps, D // steps

    def state():
        return pl.BlockSpec((1, rows, KW), lambda i: (0, i, 0))

    def flat(n, m):
        return pl.BlockSpec((n, m), lambda i: (i, 0))

    return pl.pallas_call(
        finish_kernel,
        grid=(steps,),
        out_shape=(
            jax.ShapeDtypeStruct((TOK, D), BF16),
            jax.ShapeDtypeStruct((TOK, KW), BF16),
            jax.ShapeDtypeStruct((1, ROWS, KW), F32),
            jax.ShapeDtypeStruct((1, ROWS, KW), F32),
            jax.ShapeDtypeStruct((1, ROWS, KW), F32),
            jax.ShapeDtypeStruct((ROWS // NREP, FRAGW), F32),
            jax.ShapeDtypeStruct((ROWS // NREP, FRAGW), F32),
        ),
        in_specs=[
            pl.BlockSpec(memory_space=pltpu.SMEM),
            pl.BlockSpec((TOK, KW), lambda i: (0, 0)),
            flat(cols, KW),
            state(), state(), state(),
            flat(rows, KW), flat(rows, FRAGW), flat(toks, KW), flat(own, FRAGW), flat(own, FRAGW),
        ],
        out_specs=(
            pl.BlockSpec((TOK, cols), lambda i: (0, i)),
            flat(toks, KW),
            state(), state(), state(),
            flat(own, FRAGW), flat(own, FRAGW),
        ),
        compiler_params=pltpu.CompilerParams(
            dimension_semantics=("arbitrary",), vmem_limit_bytes=40 * 2**20
        ),
        cost_estimate=pl.CostEstimate(flops=2 * TOK * D * KW, bytes_accessed=24 * 2**20, transcendentals=0),
        name="finish",
    )(fragment, cotangent, full, inner_weight, first_moment, second_moment, grad, block, keys, outer, mom)


def local_step(tokens, cotangent, inner_weight, first_moment, second_moment, outer_params, outer_momentum, fragment):
    full, keys, grad, block, outer, mom = exchange(
        fragment, tokens, cotangent, inner_weight, first_moment, second_moment, outer_params, outer_momentum
    )
    input_grad, keys, inner_next, first_next, second_next, outer_next, mom_next = finish(
        fragment, cotangent, full.reshape(D, KW), inner_weight, first_moment, second_moment, grad, block, keys, outer, mom
    )
    return keys, input_grad, inner_next, first_next, second_next, outer_next, mom_next


def solution(mesh):
    tokens = P(("replica", "shard"), None)
    state = P("replica", "shard", None)
    owned = P(("shard", "replica"), None)
    return jax.shard_map(
        local_step,
        mesh=mesh,
        in_specs=(tokens, tokens, state, state, state, owned, owned, P()),
        out_specs=(tokens, tokens, state, state, state, owned, owned),
        check_vma=False,
    )
```

```python
import functools

import jax
import jax.numpy as jnp
from jax import lax
from jax.experimental import pallas as pl
from jax.experimental.pallas import tpu as pltpu
from jax.sharding import PartitionSpec as P

MESH = pl.DeviceIdType.MESH
BF16 = jnp.bfloat16
F32 = jnp.float32

beta_first = 0.9
beta_second = 0.95
adam_rate = 0.05
decay_rate = 0.1
adam_eps = 1e-08
correction_first = 0.9999734386011124
correction_second = 0.994079470779666
outer_rate = 0.7
outer_beta = 0.9
mixing_weight = 0.5

D, KW, FRAGW, TOK, ROWS = 8192, 512, 128, 640, 256
NSHARD, NREP = 32, 4
SCALE = D ** (-0.5)
GRAD_SCALE = (TOK * NSHARD) ** (-0.5)
NSTREAM = 4
PART = ROWS // NSTREAM

LINKS = ("x+", "x-", "z+", "z-", "y")
BACK = {"x+": "x-", "x-": "x+", "z+": "z-", "z-": "z+", "y": "y"}
ROOT = (0, 0, 0)
NODES = [(x, y, z) for z in (2, 1, 3, 0) for x in (2, 1, 3, 0) for y in (1, 0)]
TREES = (("x", 1), ("z", 1), ("x", -1), ("z", -1))

SEND_US = 1.42
HOP_US = 2.0
GRAD_US = 0.45
TILE_US = 0.5
ADD_US = 0.25
ISSUE_US = 0.05
DEPTH = 4


def tree_parent(tree, node):
    first, sign = tree
    x, y, z = node
    a, b = (x, z) if first == "x" else (z, x)
    second = "z" if first == "x" else "x"

    def back(v):
        if sign > 0:
            return {1: (0, "+"), 2: (1, "+"), 3: (0, "-")}[v]
        return {3: (0, "-"), 2: (3, "-"), 1: (0, "+")}[v]

    if b == 2 and y == 1 and a in (0, 2):
        a, y, b, link = a, 0, b, "y"
    elif b:
        b, way = back(b)
        link = second + way
    elif y:
        y, link = 0, "y"
    else:
        a, way = back(a)
        link = first + way
    return ((a, y, b) if first == "x" else (b, y, a)), link


def make_trees():
    parent, children = {}, {}
    for s, tree in enumerate(TREES):
        for node in NODES:
            children.setdefault((s, node), [])
        for node in NODES:
            if node != ROOT:
                up, link = tree_parent(tree, node)
                parent[s, node] = (up, link)
                children[s, up].append((node, link))
    return parent, children


PARENT, CHILDREN = make_trees()
EDGES = {key: i for i, key in enumerate(sorted(PARENT))}


def plan_links():
    def height(key):
        return 1 + max([height((key[0], c)) for c, _ in CHILDREN[key]], default=0)

    def depth(key):
        return 0 if key[1] == ROOT else 1 + depth((key[0], PARENT[key][0]))

    grads_done = NSHARD * GRAD_US + 3.0
    waiting = {key: len(v) for key, v in CHILDREN.items()}
    latest = {key: 0.0 for key in CHILDREN}
    ready = {link: [] for link in LINKS}
    free = {link: 0.0 for link in LINKS}
    for s in range(NSTREAM):
        for node, link in CHILDREN[s, ROOT]:
            ready[link].append((0.0, "gather", s, node))
    for key in PARENT:
        if not waiting[key]:
            ready[BACK[PARENT[key][1]]].append((grads_done, "reduce") + key)
    sends, arrival, roots, begun = [], {}, {}, {}
    while any(ready.values()):
        at, link = min((max(free[k], min(r[0] for r in v)), k) for k, v in ready.items() if v)
        open_now = [r for r in ready[link] if r[0] <= at + 1e-9]

        def rank(r):
            key = r[2:]
            if r[1] == "reduce":
                return (1, depth(key), 0, -EDGES[key])
            return (0, height(key) + begun.get(key[1], 0), 0, -EDGES[key])

        pick = max(open_now, key=rank)
        ready[link].remove(pick)
        _, kind, s, node = pick
        free[link] = at + SEND_US
        there = at + SEND_US + HOP_US
        sends.append((at, link, kind, s, node))
        arrival[kind, s, node] = there
        if kind == "gather":
            begun[node] = begun.get(node, 0) + 1
            for child, way in CHILDREN[s, node]:
                ready[way].append((there, "gather", s, child))
        else:
            up = (s, PARENT[s, node][0])
            waiting[up] -= 1
            latest[up] = max(latest[up], there)
            if not waiting[up]:
                if up[1] == ROOT:
                    roots[s] = latest[up]
                else:
                    ready[BACK[PARENT[up][1]]].append((max(latest[up] + ADD_US, grads_done), "reduce") + up)
    return sends, arrival, max(roots.values())


def make_program():
    sends, arrival, roots_at = plan_links()
    full_at = {n: max(arrival["gather", s, n] for s in range(NSTREAM)) for n in NODES if n != ROOT}
    full_at[ROOT] = 0.0
    tiles_left = sorted(NODES, key=lambda n: full_at[n])
    tail = [(roots_at, "update"), (roots_at + 6.0, "outer"), (roots_at + 12.0, "spread")]
    events = sorted([(t, 1, ("send",) + tuple(r)) for t, *r in sends] + [(t, 0, (n,)) for t, n in tail], key=lambda e: e[:2])
    program, now, grads = [], 0.0, 0
    for at, _, op in events:
        while True:
            if grads < NSHARD and (now + 0.5 * GRAD_US < at or op[0] != "send" or op[2] == "reduce"):
                program.append(("grad", grads))
                grads += 1
                now += GRAD_US
            elif grads == NSHARD and tiles_left and full_at[tiles_left[0]] < now and now + 0.5 * TILE_US < at:
                program.append(("tile", tiles_left.pop(0)))
                now += TILE_US
            else:
                break
        now = max(now, at) + (ADD_US if op[0] == "send" and op[2] == "reduce" else ISSUE_US)
        program.append(op)
    program += [("tile", n) for n in tiles_left]
    return program


def adam(weight, grad, first, second):
    first_next = beta_first * first + (1.0 - beta_first) * grad
    second_next = beta_second * second + (1.0 - beta_second) * grad * grad
    step = first_next / correction_first / (jnp.sqrt(second_next / correction_second) + adam_eps)
    return weight - adam_rate * (step + decay_rate * weight), first_next, second_next


def select_block(fragment, array):
    block = array[:, :FRAGW]
    for f in range(1, KW // FRAGW):
        block = jnp.where(fragment == f, array[:, f * FRAGW : (f + 1) * FRAGW], block)
    return block


def exchange_kernel(
    fragment_ref, tokens_hbm, cot_hbm, weight_hbm, first_hbm, second_hbm, outer_hbm, mom_hbm,
    keys_ref, input_ref, inner_ref, first_ref, second_ref, outer_ref, mom_ref,
    tokens, cot, weight, first, second, outer, mom, full, sums, landed, keys_acc, grad, inner, peers, spread,
    in_sem, send_sem, gather_sem, reduce_sem, peer_send, peer_recv, spread_send, spread_recv,
):
    shard, rep = lax.axis_index("shard"), lax.axis_index("replica")
    my, mx, mz = shard % 2, (shard // 2) % 4, shard // 8
    core, high = rep % 2, rep // 2

    def owner(node):
        x, y, z = node
        return (((mz + 4 - z) % 4) * 4 + (mx + 4 - x) % 4) * 2 + (my + y) % 2

    def shard_at(link):
        x, y, z = mx, my, mz
        if link == "y":
            y = 1 - y
        elif link[0] == "x":
            x = (x + (1 if link[1] == "+" else 3)) % 4
        else:
            z = (z + (1 if link[1] == "+" else 3)) % 4
        return (z * 4 + x) * 2 + y

    there = {link: {"shard": shard_at(link)} for link in LINKS}
    peer = [high * 2 + 1 - core, (1 - high) * 2 + core, (1 - high) * 2 + 1 - core]

    def local(src, dst, i):
        return pltpu.make_async_copy(src, dst, in_sem.at[i])

    loads = [
        local(weight_hbm.at[0], weight, 0),
        local(cot_hbm, cot, 1),
        local(tokens_hbm, tokens, 2),
        local(first_hbm.at[0], first, 3),
        local(second_hbm.at[0], second, 4),
        local(outer_hbm, outer, 5),
        local(mom_hbm, mom, 6),
    ]
    for copy in loads:
        copy.start()
    barrier = pltpu.get_barrier_semaphore()
    for link in LINKS:
        pl.semaphore_signal(barrier, inc=1, device_id=there[link], device_id_type=MESH)
    for p in peer:
        pl.semaphore_signal(barrier, inc=1, device_id={"replica": p}, device_id_type=MESH)
    loads[0].wait()
    full[shard] = weight[...].astype(BF16)
    pl.semaphore_wait(barrier, 8)

    def part(s):
        return pl.ds(s * PART, PART)

    issued = {link: [] for link in LINKS}
    waited = set()

    def send_copy(kind, s, node, slot):
        edge = EDGES[s, node]
        up, link = PARENT[s, node]
        if kind == "gather":
            where = full.at[owner(up), part(s)]
            return pltpu.make_async_remote_copy(
                src_ref=where, dst_ref=where, send_sem=send_sem.at[LINKS.index(link), slot],
                recv_sem=gather_sem.at[edge], device_id=there[link], device_id_type=MESH,
            )
        link = BACK[link]
        return pltpu.make_async_remote_copy(
            src_ref=sums.at[owner(node), part(s)], dst_ref=landed.at[edge],
            send_sem=send_sem.at[LINKS.index(link), slot],
            recv_sem=reduce_sem.at[edge], device_id=there[link], device_id_type=MESH,
        )

    def arrived(kind, s, node):
        if (kind, s, node) in waited or node == ROOT:
            return
        waited.add((kind, s, node))
        edge = EDGES[s, node]
        if kind == "gather":
            where = full.at[owner(node), part(s)]
            pltpu.make_async_copy(where, where, gather_sem.at[edge]).wait()
        else:
            where = landed.at[edge]
            pltpu.make_async_copy(where, where, reduce_sem.at[edge]).wait()

    def summed(s, node):
        total = sums[owner(node), part(s)].astype(F32)
        for child, _ in CHILDREN[s, node]:
            arrived("reduce", s, child)
            total = total + landed[EDGES[s, child]].astype(F32)
        return total

    def send(link, kind, s, node):
        if kind == "gather":
            arrived("gather", s, PARENT[s, node][0])
        elif CHILDREN[s, node]:
            sums[owner(node), part(s)] = summed(s, node).astype(BF16)
        line = issued[link]
        if len(line) >= DEPTH:
            line[-DEPTH].wait_send()
        copy = send_copy(kind, s, node, len(line) % DEPTH)
        copy.start()
        line.append(copy)

    def grad_tile(i, carry):
        z, x, y = (2 + i // 8) % 4, (2 + (i % 8) // 2) % 4, 1 - i % 2
        which = owner((x, y, z))
        cols = pl.ds(pl.multiple_of(which * ROWS, ROWS), ROWS)
        sums[which] = lax.dot_general(
            tokens[:, cols], cot[...], (((0,), (0,)), ((), ())), preferred_element_type=F32
        ).astype(BF16)
        return carry

    def weight_tile(node, begin):
        for s in range(NSTREAM):
            arrived("gather", s, node)
        which = owner(node)
        cols = pl.ds(pl.multiple_of(which * ROWS, ROWS), ROWS)
        term = jnp.dot(tokens[:, cols], full[which], preferred_element_type=F32)
        if begin:
            keys_acc[...] = term
        else:
            keys_acc[...] += term
        back = lax.dot_general(cot[...], full[which], (((1,), (1,)), ((), ())), preferred_element_type=F32)
        input_ref[:, cols] = (back * SCALE).astype(BF16)

    mine = pl.ds(pl.multiple_of(rep * (ROWS // NREP), ROWS // NREP), ROWS // NREP)

    def update():
        for s in range(NSTREAM):
            grad[part(s), :] = summed(s, ROOT) * GRAD_SCALE
        for copy in loads[3:]:
            copy.wait()
        f = fragment_ref[0]
        inner[...] = adam(
            select_block(f, weight[...]), select_block(f, grad[...]),
            select_block(f, first[...]), select_block(f, second[...]),
        )[0]
        for copy in to_peers():
            copy.start()
        inner_ref[0], first_ref[0], second_ref[0] = adam(weight[...], grad[...], first[...], second[...])

    def to_peers():
        return [
            pltpu.make_async_remote_copy(
                src_ref=inner.at[pl.ds(pl.multiple_of(p * (ROWS // NREP), ROWS // NREP), ROWS // NREP)],
                dst_ref=peers.at[k], send_sem=peer_send.at[k], recv_sem=peer_recv.at[k],
                device_id={"replica": p}, device_id_type=MESH,
            )
            for k, p in enumerate(peer)
        ]

    def to_all():
        return [
            pltpu.make_async_remote_copy(
                src_ref=spread.at[mine], dst_ref=spread.at[mine], send_sem=spread_send.at[k],
                recv_sem=spread_recv.at[k], device_id={"replica": p}, device_id_type=MESH,
            )
            for k, p in enumerate(peer)
        ]

    def outer_step():
        total = inner[mine]
        for k, copy in enumerate(to_peers()):
            copy.wait_recv()
            total = total + peers[k]
        pseudo = outer[...] - total / NREP
        mom_next = outer_beta * mom[...] + pseudo
        outer_next = outer[...] - outer_rate * (pseudo + outer_beta * mom_next)
        outer_ref[...] = outer_next
        mom_ref[...] = mom_next
        spread[mine] = outer_next
        for copy in to_all():
            copy.start()

    def spread_step():
        for k, p in enumerate(peer):
            rows = pl.ds(pl.multiple_of(p * (ROWS // NREP), ROWS // NREP), ROWS // NREP)
            pltpu.make_async_copy(spread.at[rows], spread.at[rows], spread_recv.at[k]).wait()
        mixed = mixing_weight * inner[...] + (1.0 - mixing_weight) * spread[...]
        for f in range(KW // FRAGW):
            cols = slice(f * FRAGW, (f + 1) * FRAGW)
            inner_ref[0, :, cols] = jnp.where(fragment_ref[0] == f, mixed, inner_ref[0, :, cols])

    program = make_program()
    at, begin = 0, True
    while at < len(program):
        op = program[at]
        if op[0] == "grad":
            if op[1] == 0:
                loads[1].wait()
                loads[2].wait()
            n = 1
            while at + n < len(program) and program[at + n][0] == "grad":
                n += 1
            lax.fori_loop(op[1], op[1] + n, grad_tile, 0)
            at += n
            continue
        if op[0] == "send":
            send(*op[1:])
        elif op[0] == "tile":
            weight_tile(op[1], begin)
            begin = False
        else:
            {"update": update, "outer": outer_step, "spread": spread_step}[op[0]]()
        at += 1

    keys_ref[...] = (keys_acc[...] * SCALE).astype(BF16)
    for line in issued.values():
        for copy in line[-DEPTH:]:
            copy.wait_send()
    for copy in to_peers() + to_all():
        copy.wait_send()


def finish_kernel(*refs):
    half = (len(refs) - 1) // 2
    sems = refs[-1]
    copies = []
    for src, dst in zip(refs[:half], refs[half:-1]):
        cuts = 4 if src.size > 2**20 else 1
        rows = src.shape[0] // cuts
        for c in range(cuts):
            where = pl.ds(c * rows, rows)
            copies.append(pltpu.make_async_copy(src.at[where], dst.at[where], sems.at[len(copies)]))
            copies[-1].start()
    for copy in copies:
        copy.wait()


OUTS = (
    ((TOK, KW), BF16),
    ((TOK, D), BF16),
    ((1, ROWS, KW), F32),
    ((1, ROWS, KW), F32),
    ((1, ROWS, KW), F32),
    ((ROWS // NREP, FRAGW), F32),
    ((ROWS // NREP, FRAGW), F32),
)


def exchange(fragment, tokens, cotangent, inner_weight, first_moment, second_moment, outer_params, outer_momentum):
    anyspace = pl.BlockSpec(memory_space=pl.ANY)
    vmem = pl.BlockSpec(memory_space=pltpu.VMEM)
    edges = len(EDGES)
    return pl.pallas_call(
        exchange_kernel,
        out_shape=[pltpu.VMEM(shape, dtype) for shape, dtype in OUTS],
        in_specs=[pl.BlockSpec(memory_space=pltpu.SMEM)] + [anyspace] * 7,
        out_specs=[vmem] * len(OUTS),
        scratch_shapes=[
            pltpu.VMEM((TOK, D), BF16),
            pltpu.VMEM((TOK, KW), BF16),
            pltpu.VMEM((ROWS, KW), F32),
            pltpu.VMEM((ROWS, KW), F32),
            pltpu.VMEM((ROWS, KW), F32),
            pltpu.VMEM((ROWS // NREP, FRAGW), F32),
            pltpu.VMEM((ROWS // NREP, FRAGW), F32),
            pltpu.VMEM((NSHARD, ROWS, KW), BF16),
            pltpu.VMEM((NSHARD, ROWS, KW), BF16),
            pltpu.VMEM((edges, PART, KW), BF16),
            pltpu.VMEM((TOK, KW), F32),
            pltpu.VMEM((ROWS, KW), F32),
            pltpu.VMEM((ROWS, FRAGW), F32),
            pltpu.VMEM((NREP - 1, ROWS // NREP, FRAGW), F32),
            pltpu.VMEM((ROWS, FRAGW), F32),
            pltpu.SemaphoreType.DMA((7,)),
            pltpu.SemaphoreType.DMA((len(LINKS), DEPTH)),
            pltpu.SemaphoreType.DMA((edges,)),
            pltpu.SemaphoreType.DMA((edges,)),
            pltpu.SemaphoreType.DMA((NREP - 1,)),
            pltpu.SemaphoreType.DMA((NREP - 1,)),
            pltpu.SemaphoreType.DMA((NREP - 1,)),
            pltpu.SemaphoreType.DMA((NREP - 1,)),
        ],
        compiler_params=pltpu.CompilerParams(
            collective_id=0, has_side_effects=True, vmem_limit_bytes=46 * 2**20
        ),
        cost_estimate=pl.CostEstimate(
            flops=6 * TOK * D * KW, bytes_accessed=30 * 2**20, transcendentals=0
        ),
        name="exchange",
    )(fragment, tokens, cotangent, inner_weight, first_moment, second_moment, outer_params, outer_momentum)


def finish(*arrays):
    return pl.pallas_call(
        finish_kernel,
        out_shape=[pltpu.HBM(a.shape, a.dtype) for a in arrays],
        in_specs=[pl.BlockSpec(memory_space=pltpu.VMEM)] * len(arrays),
        out_specs=[pl.BlockSpec(memory_space=pltpu.HBM)] * len(arrays),
        scratch_shapes=[pltpu.SemaphoreType.DMA((16,))],
        compiler_params=pltpu.CompilerParams(vmem_limit_bytes=2 * 2**20),
        cost_estimate=pl.CostEstimate(flops=0, bytes_accessed=13 * 2**20, transcendentals=0),
        name="finish",
    )(*[pltpu.with_memory_space_constraint(a, pltpu.VMEM) for a in arrays])


def local_step(tokens, cotangent, inner_weight, first_moment, second_moment, outer_params, outer_momentum, fragment):
    outs = exchange(
        fragment, tokens, cotangent, inner_weight, first_moment, second_moment, outer_params, outer_momentum
    )
    return tuple(finish(*outs))


def solution(mesh):
    tokens = P(("replica", "shard"), None)
    state = P("replica", "shard", None)
    owned = P(("shard", "replica"), None)
    return jax.shard_map(
        local_step,
        mesh=mesh,
        in_specs=(tokens, tokens, state, state, state, owned, owned, P()),
        out_specs=(tokens, tokens, state, state, state, owned, owned),
        check_vma=False,
    )
```

```python
import functools

import jax
import jax.numpy as jnp
from jax import lax
from jax.experimental import pallas as pl
from jax.experimental.pallas import tpu as pltpu
from jax.sharding import PartitionSpec as P

MESH = pl.DeviceIdType.MESH
BF16 = jnp.bfloat16
F32 = jnp.float32

beta_first = 0.9
beta_second = 0.95
adam_rate = 0.05
decay_rate = 0.1
adam_eps = 1e-08
correction_first = 0.9999734386011124
correction_second = 0.994079470779666
outer_rate = 0.7
outer_beta = 0.9
mixing_weight = 0.5

D, KW, FRAGW, TOK, ROWS = 8192, 512, 128, 640, 256
NSHARD, NREP = 32, 4
SCALE = D ** (-0.5)
GRAD_SCALE = (TOK * NSHARD) ** (-0.5)
NSTREAM = 4
PART = ROWS // NSTREAM

LINKS = ("x+", "x-", "z+", "z-", "y")
BACK = {"x+": "x-", "x-": "x+", "z+": "z-", "z-": "z+", "y": "y"}
ROOT = (0, 0, 0)
NODES = [(x, y, z) for z in (2, 3, 0, 1) for x in (2, 3, 0, 1) for y in (1, 0)]
TREES = (("x", 1), ("z", 1), ("x", -1), ("z", -1))

SEND_US = 1.42
HOP_US = 4.5
LOAD_US = 4.0
GRAD_US = 0.42
GRAD_SLACK = 1.0
TILE_US = 0.55
TILE_SLACK = 0.6
BACKLOG = 3
ADD_US = 0.06
ISSUE_US = 0.05
REDUCE_FROM = 8.0
GATHER_FROM = 99.0
GATHER_TO = 99.0
NEAR = 1.0
MIX = 0.0
SEED = 0
DEPTH = 4


def tree_parent(tree, node):
    first, sign = tree
    x, y, z = node
    a, b = (x, z) if first == "x" else (z, x)
    second = "z" if first == "x" else "x"

    def back(v):
        if sign > 0:
            return {1: (0, "+"), 2: (1, "+"), 3: (0, "-")}[v]
        return {3: (0, "-"), 2: (3, "-"), 1: (0, "+")}[v]

    if b == 2 and y == 1 and a in (0, 2):
        a, y, b, link = a, 0, b, "y"
    elif b:
        b, way = back(b)
        link = second + way
    elif y:
        y, link = 0, "y"
    else:
        a, way = back(a)
        link = first + way
    return ((a, y, b) if first == "x" else (b, y, a)), link


def make_trees():
    parent, children = {}, {}
    for s, tree in enumerate(TREES):
        for node in NODES:
            children.setdefault((s, node), [])
        for node in NODES:
            if node != ROOT:
                up, link = tree_parent(tree, node)
                parent[s, node] = (up, link)
                children[s, up].append((node, link))
    return parent, children


PARENT, CHILDREN = make_trees()
EDGES = {key: i for i, key in enumerate(sorted(PARENT))}


def plan_links():
    def height(key):
        return 1 + max([height((key[0], c)) for c, _ in CHILDREN[key]], default=0)

    def depth(key):
        return 0 if key[1] == ROOT else 1 + depth((key[0], PARENT[key][0]))

    grad_at = {node: LOAD_US + GRAD_US * GRAD_SLACK * (i + 1) for i, node in enumerate(NODES)}
    waiting = {key: len(v) for key, v in CHILDREN.items()}
    latest = {key: grad_at[key[1]] for key in CHILDREN}
    ready = {link: [] for link in LINKS}
    free = {link: 0.0 for link in LINKS}
    for s in range(NSTREAM):
        for node, link in CHILDREN[s, ROOT]:
            ready[link].append((0.0, "gather", s, node))
    for key in PARENT:
        if not waiting[key]:
            ready[BACK[PARENT[key][1]]].append((latest[key], "reduce") + key)
    sends, arrival, roots, begun = [], {}, {}, {}
    while any(ready.values()):
        at, link = min((max(free[k], min(r[0] for r in v)), k) for k, v in ready.items() if v)
        open_now = [r for r in ready[link] if r[0] <= at + 1e-9]

        def rank(r):
            key = r[2:]
            mixed = MIX * ((EDGES[key] * 37 + SEED) % 101) / 101
            if r[1] == "reduce":
                first = REDUCE_FROM <= at and not GATHER_FROM <= at < GATHER_TO
                return (1 if first else -1, depth(key) + mixed, -r[0], -EDGES[key])
            return (0, height(key) + NEAR * begun.get(key[1], 0) + mixed, -r[0], -EDGES[key])

        pick = max(open_now, key=rank)
        ready[link].remove(pick)
        _, kind, s, node = pick
        free[link] = at + SEND_US
        there = at + SEND_US + HOP_US
        sends.append((at, link, kind, s, node))
        arrival[kind, s, node] = there
        if kind == "gather":
            begun[node] = begun.get(node, 0) + 1
            for child, way in CHILDREN[s, node]:
                ready[way].append((there, "gather", s, child))
        else:
            up = (s, PARENT[s, node][0])
            waiting[up] -= 1
            latest[up] = max(latest[up], there)
            if not waiting[up]:
                if up[1] == ROOT:
                    roots[s] = latest[up]
                else:
                    ready[BACK[PARENT[up][1]]].append((latest[up] + ADD_US, "reduce") + up)
    return sends, arrival, max(roots.values())


def make_program():
    sends, arrival, roots_at = plan_links()
    full_at = {n: max(arrival["gather", s, n] for s in range(NSTREAM)) for n in NODES if n != ROOT}
    full_at[ROOT] = 0.0
    tiles_left = sorted(NODES, key=lambda n: full_at[n])
    order = {node: i for i, node in enumerate(NODES)}
    tail = [(roots_at, "update"), (roots_at + 6.0, "outer"), (roots_at + 12.0, "spread")]
    events = sorted([(t, 1, ("send",) + tuple(r)) for t, *r in sends] + [(t, 0, (n,)) for t, n in tail], key=lambda e: e[:2])
    program, now, grads = [], 0.0, 0
    for at, _, op in events:
        need = order[op[3 + 1]] + 1 if op[0] == "send" and op[2] == "reduce" else 0
        while True:
            if grads < max(need, NSHARD * (op[0] != "send")):
                pass
            elif grads < NSHARD and max(now, LOAD_US) + 0.5 * GRAD_US < at:
                pass
            elif grads == NSHARD and tiles_left and full_at[tiles_left[0]] < now:
                backlog = sum(full_at[n] < now for n in tiles_left)
                if now + TILE_SLACK * TILE_US < at or backlog > BACKLOG:
                    program.append(("tile", tiles_left.pop(0)))
                    now += TILE_US
                    continue
                break
            else:
                break
            program.append(("grad", grads))
            now = max(now, LOAD_US) + GRAD_US
            grads += 1
        now = max(now, at) + (ADD_US if op[0] == "send" and op[2] == "reduce" else ISSUE_US)
        program.append(op)
    program += [("tile", n) for n in tiles_left]
    return program


def adam(weight, grad, first, second):
    first_next = beta_first * first + (1.0 - beta_first) * grad
    second_next = beta_second * second + (1.0 - beta_second) * grad * grad
    step = first_next / correction_first / (jnp.sqrt(second_next / correction_second) + adam_eps)
    return weight - adam_rate * (step + decay_rate * weight), first_next, second_next


def select_block(fragment, array):
    block = array[:, :FRAGW]
    for f in range(1, KW // FRAGW):
        block = jnp.where(fragment == f, array[:, f * FRAGW : (f + 1) * FRAGW], block)
    return block


def exchange_kernel(
    fragment_hbm, tokens_hbm, cot_hbm, weight_hbm, first_hbm, second_hbm, outer_hbm, mom_hbm,
    keys_ref, input_ref, inner_ref, first_ref, second_ref, outer_ref, mom_ref,
    fragment_ref, tokens, cot, weight, first, second, outer, mom, full, sums, landed, keys_acc, grad, inner, peers, spread,
    in_sem, send_sem, gather_sem, reduce_sem, peer_send, peer_recv, spread_send, spread_recv, ready,
):
    shard, rep = lax.axis_index("shard"), lax.axis_index("replica")
    my, mx, mz = shard % 2, (shard // 2) % 4, shard // 8
    core, high = rep % 2, rep // 2

    def owner(node):
        x, y, z = node
        return (((mz + 4 - z) % 4) * 4 + (mx + 4 - x) % 4) * 2 + (my + y) % 2

    def shard_at(link):
        x, y, z = mx, my, mz
        if link == "y":
            y = 1 - y
        elif link[0] == "x":
            x = (x + (1 if link[1] == "+" else 3)) % 4
        else:
            z = (z + (1 if link[1] == "+" else 3)) % 4
        return (z * 4 + x) * 2 + y

    there = {link: {"shard": shard_at(link)} for link in LINKS}
    peer = [high * 2 + 1 - core, (1 - high) * 2 + core, (1 - high) * 2 + 1 - core]

    def local(src, dst, i):
        return pltpu.make_async_copy(src, dst, in_sem.at[i])

    loads = [
        local(weight_hbm.at[0], weight, 0),
        local(cot_hbm, cot, 1),
        local(tokens_hbm, tokens, 2),
        local(first_hbm.at[0], first, 3),
        local(second_hbm.at[0], second, 4),
        local(outer_hbm, outer, 5),
        local(mom_hbm, mom, 6),
        local(fragment_hbm, fragment_ref, 7),
    ]
    loads[0].start()
    barrier = pltpu.get_barrier_semaphore()
    for link in LINKS:
        pl.semaphore_signal(barrier, inc=1, device_id=there[link], device_id_type=MESH)
    for p in peer:
        @pl.when(p > rep)
        def _():
            pl.semaphore_signal(barrier, inc=1, device_id={"replica": p}, device_id_type=MESH)

    loads[0].wait()
    for copy in loads[1:]:
        copy.start()
    full[shard] = weight[...].astype(BF16)
    pl.semaphore_wait(barrier, len(LINKS) + rep)
    for p in peer:
        @pl.when(p < rep)
        def _():
            pl.semaphore_signal(ready, inc=1, device_id={"replica": p}, device_id_type=MESH)


    def part(s):
        return pl.ds(s * PART, PART)

    issued = {link: [] for link in LINKS}
    waited = set()

    def send_copy(kind, s, node, slot):
        edge = EDGES[s, node]
        up, link = PARENT[s, node]
        if kind == "gather":
            where = full.at[owner(up), part(s)]
            return pltpu.make_async_remote_copy(
                src_ref=where, dst_ref=where, send_sem=send_sem.at[LINKS.index(link), slot],
                recv_sem=gather_sem.at[edge], device_id=there[link], device_id_type=MESH,
            )
        link = BACK[link]
        return pltpu.make_async_remote_copy(
            src_ref=sums.at[owner(node), part(s)], dst_ref=landed.at[edge],
            send_sem=send_sem.at[LINKS.index(link), slot],
            recv_sem=reduce_sem.at[edge], device_id=there[link], device_id_type=MESH,
        )

    def arrived(kind, s, node):
        if (kind, s, node) in waited or node == ROOT:
            return
        waited.add((kind, s, node))
        edge = EDGES[s, node]
        if kind == "gather":
            where = full.at[owner(node), part(s)]
            pltpu.make_async_copy(where, where, gather_sem.at[edge]).wait()
        else:
            where = landed.at[edge]
            pltpu.make_async_copy(where, where, reduce_sem.at[edge]).wait()

    def summed(s, node):
        total = sums[owner(node), part(s)].astype(F32)
        for child, _ in CHILDREN[s, node]:
            arrived("reduce", s, child)
            total = total + landed[EDGES[s, child]].astype(F32)
        return total

    def send(link, kind, s, node):
        if kind == "gather":
            arrived("gather", s, PARENT[s, node][0])
        elif CHILDREN[s, node]:
            sums[owner(node), part(s)] = summed(s, node).astype(BF16)
        line = issued[link]
        if len(line) >= DEPTH:
            line[-DEPTH].wait_send()
        copy = send_copy(kind, s, node, len(line) % DEPTH)
        copy.start()
        line.append(copy)

    def grad_tile(i, carry):
        z, x, y = (2 + i // 8) % 4, (2 + (i % 8) // 2) % 4, 1 - i % 2
        which = owner((x, y, z))
        cols = pl.ds(pl.multiple_of(which * ROWS, ROWS), ROWS)
        sums[which] = lax.dot_general(
            tokens[:, cols], cot[...], (((0,), (0,)), ((), ())), preferred_element_type=F32
        ).astype(BF16)
        return carry

    def weight_tile(node, begin):
        for s in range(NSTREAM):
            arrived("gather", s, node)
        which = owner(node)
        cols = pl.ds(pl.multiple_of(which * ROWS, ROWS), ROWS)
        term = jnp.dot(tokens[:, cols], full[which], preferred_element_type=F32)
        if begin:
            keys_acc[...] = term
        else:
            keys_acc[...] += term
        back = lax.dot_general(cot[...], full[which], (((1,), (1,)), ((), ())), preferred_element_type=F32)
        input_ref[:, cols] = (back * SCALE).astype(BF16)

    mine = pl.ds(pl.multiple_of(rep * (ROWS // NREP), ROWS // NREP), ROWS // NREP)

    def update():
        for s in range(NSTREAM):
            grad[part(s), :] = summed(s, ROOT) * GRAD_SCALE
        for copy in loads[3:]:
            copy.wait()
        f = fragment_ref[0]
        inner[...] = adam(
            select_block(f, weight[...]), select_block(f, grad[...]),
            select_block(f, first[...]), select_block(f, second[...]),
        )[0]

        @pl.when(rep < NREP - 1)
        def _():
            pl.semaphore_wait(ready, NREP - 1 - rep)

        for copy in to_peers():
            copy.start()
        inner_ref[0], first_ref[0], second_ref[0] = adam(weight[...], grad[...], first[...], second[...])

    def to_peers():
        return [
            pltpu.make_async_remote_copy(
                src_ref=inner.at[pl.ds(pl.multiple_of(p * (ROWS // NREP), ROWS // NREP), ROWS // NREP)],
                dst_ref=peers.at[k], send_sem=peer_send.at[k], recv_sem=peer_recv.at[k],
                device_id={"replica": p}, device_id_type=MESH,
            )
            for k, p in enumerate(peer)
        ]

    def to_all():
        return [
            pltpu.make_async_remote_copy(
                src_ref=spread.at[mine], dst_ref=spread.at[mine], send_sem=spread_send.at[k],
                recv_sem=spread_recv.at[k], device_id={"replica": p}, device_id_type=MESH,
            )
            for k, p in enumerate(peer)
        ]

    def outer_step():
        total = inner[mine]
        for k, copy in enumerate(to_peers()):
            copy.wait_recv()
            total = total + peers[k]
        pseudo = outer[...] - total / NREP
        mom_next = outer_beta * mom[...] + pseudo
        outer_next = outer[...] - outer_rate * (pseudo + outer_beta * mom_next)
        outer_ref[...] = outer_next
        mom_ref[...] = mom_next
        spread[mine] = outer_next
        for copy in to_all():
            copy.start()

    def spread_step():
        for k, p in enumerate(peer):
            rows = pl.ds(pl.multiple_of(p * (ROWS // NREP), ROWS // NREP), ROWS // NREP)
            pltpu.make_async_copy(spread.at[rows], spread.at[rows], spread_recv.at[k]).wait()
        mixed = mixing_weight * inner[...] + (1.0 - mixing_weight) * spread[...]
        for f in range(KW // FRAGW):
            cols = slice(f * FRAGW, (f + 1) * FRAGW)
            inner_ref[0, :, cols] = jnp.where(fragment_ref[0] == f, mixed, inner_ref[0, :, cols])

    program = make_program()
    at, begin = 0, True
    while at < len(program):
        op = program[at]
        if op[0] == "grad":
            if op[1] == 0:
                loads[1].wait()
                loads[2].wait()
            n = 1
            while at + n < len(program) and program[at + n][0] == "grad":
                n += 1
            lax.fori_loop(op[1], op[1] + n, grad_tile, 0)
            at += n
            continue
        if op[0] == "send":
            send(*op[1:])
        elif op[0] == "tile":
            weight_tile(op[1], begin)
            begin = False
        else:
            {"update": update, "outer": outer_step, "spread": spread_step}[op[0]]()
        at += 1

    keys_ref[...] = (keys_acc[...] * SCALE).astype(BF16)
    for line in issued.values():
        for copy in line[-DEPTH:]:
            copy.wait_send()
    for copy in to_peers() + to_all():
        copy.wait_send()


def finish_kernel(*refs):
    half = (len(refs) - 1) // 2
    sems = refs[-1]
    copies = []
    for src, dst in zip(refs[:half], refs[half:-1]):
        cuts = 4 if src.size > 2**20 else 1
        rows = src.shape[0] // cuts
        for c in range(cuts):
            where = pl.ds(c * rows, rows)
            copies.append(pltpu.make_async_copy(src.at[where], dst.at[where], sems.at[len(copies)]))
            copies[-1].start()
    for copy in copies:
        copy.wait()


OUTS = (
    ((TOK, KW), BF16),
    ((TOK, D), BF16),
    ((1, ROWS, KW), F32),
    ((1, ROWS, KW), F32),
    ((1, ROWS, KW), F32),
    ((ROWS // NREP, FRAGW), F32),
    ((ROWS // NREP, FRAGW), F32),
)


def exchange(fragment, tokens, cotangent, inner_weight, first_moment, second_moment, outer_params, outer_momentum):
    anyspace = pl.BlockSpec(memory_space=pl.ANY)
    vmem = pl.BlockSpec(memory_space=pltpu.VMEM)
    edges = len(EDGES)
    return pl.pallas_call(
        exchange_kernel,
        out_shape=[pltpu.VMEM(shape, dtype) for shape, dtype in OUTS],
        in_specs=[anyspace] * 8,
        out_specs=[vmem] * len(OUTS),
        scratch_shapes=[
            pltpu.SMEM((1,), jnp.int32),
            pltpu.VMEM((TOK, D), BF16),
            pltpu.VMEM((TOK, KW), BF16),
            pltpu.VMEM((ROWS, KW), F32),
            pltpu.VMEM((ROWS, KW), F32),
            pltpu.VMEM((ROWS, KW), F32),
            pltpu.VMEM((ROWS // NREP, FRAGW), F32),
            pltpu.VMEM((ROWS // NREP, FRAGW), F32),
            pltpu.VMEM((NSHARD, ROWS, KW), BF16),
            pltpu.VMEM((NSHARD, ROWS, KW), BF16),
            pltpu.VMEM((edges, PART, KW), BF16),
            pltpu.VMEM((TOK, KW), F32),
            pltpu.VMEM((ROWS, KW), F32),
            pltpu.VMEM((ROWS, FRAGW), F32),
            pltpu.VMEM((NREP - 1, ROWS // NREP, FRAGW), F32),
            pltpu.VMEM((ROWS, FRAGW), F32),
            pltpu.SemaphoreType.DMA((8,)),
            pltpu.SemaphoreType.DMA((len(LINKS), DEPTH)),
            pltpu.SemaphoreType.DMA((edges,)),
            pltpu.SemaphoreType.DMA((edges,)),
            pltpu.SemaphoreType.DMA((NREP - 1,)),
            pltpu.SemaphoreType.DMA((NREP - 1,)),
            pltpu.SemaphoreType.DMA((NREP - 1,)),
            pltpu.SemaphoreType.DMA((NREP - 1,)),
            pltpu.SemaphoreType.REGULAR,
        ],
        compiler_params=pltpu.CompilerParams(
            collective_id=0, has_side_effects=True, vmem_limit_bytes=46 * 2**20
        ),
        cost_estimate=pl.CostEstimate(
            flops=6 * TOK * D * KW, bytes_accessed=30 * 2**20, transcendentals=0
        ),
        name="exchange",
    )(fragment, tokens, cotangent, inner_weight, first_moment, second_moment, outer_params, outer_momentum)


def finish(*arrays):
    return pl.pallas_call(
        finish_kernel,
        out_shape=[pltpu.HBM(a.shape, a.dtype) for a in arrays],
        in_specs=[pl.BlockSpec(memory_space=pltpu.VMEM)] * len(arrays),
        out_specs=[pl.BlockSpec(memory_space=pltpu.HBM)] * len(arrays),
        scratch_shapes=[pltpu.SemaphoreType.DMA((16,))],
        compiler_params=pltpu.CompilerParams(vmem_limit_bytes=2 * 2**20),
        cost_estimate=pl.CostEstimate(flops=0, bytes_accessed=13 * 2**20, transcendentals=0),
        name="finish",
    )(*[pltpu.with_memory_space_constraint(a, pltpu.VMEM) for a in arrays])


def local_step(tokens, cotangent, inner_weight, first_moment, second_moment, outer_params, outer_momentum, fragment):
    outs = exchange(
        fragment, tokens, cotangent, inner_weight, first_moment, second_moment, outer_params, outer_momentum
    )
    return tuple(finish(*outs))


def solution(mesh):
    tokens = P(("replica", "shard"), None)
    state = P("replica", "shard", None)
    owned = P(("shard", "replica"), None)
    return jax.shard_map(
        local_step,
        mesh=mesh,
        in_specs=(tokens, tokens, state, state, state, owned, owned, P()),
        out_specs=(tokens, tokens, state, state, state, owned, owned),
        check_vma=False,
    )
```

```python
import functools

import jax
import jax.numpy as jnp
from jax import lax
from jax.experimental import pallas as pl
from jax.experimental.pallas import tpu as pltpu
from jax.sharding import PartitionSpec as P

MESH = pl.DeviceIdType.MESH
BF16 = jnp.bfloat16
F32 = jnp.float32

beta_first = 0.9
beta_second = 0.95
adam_rate = 0.05
decay_rate = 0.1
adam_eps = 1e-08
correction_first = 0.9999734386011124
correction_second = 0.994079470779666
outer_rate = 0.7
outer_beta = 0.9
mixing_weight = 0.5

D, KW, FRAGW, TOK, ROWS = 8192, 512, 128, 640, 256
NSHARD, NREP = 32, 4
SCALE = D ** (-0.5)
GRAD_SCALE = (TOK * NSHARD) ** (-0.5)
NSTREAM = 4
PART = ROWS // NSTREAM

LINKS = ("x+", "x-", "z+", "z-", "y")
BACK = {"x+": "x-", "x-": "x+", "z+": "z-", "z-": "z+", "y": "y"}
ROOT = (0, 0, 0)
ORDER = (2, 1, 3, 0)
NODES = [(x, y, z) for z in ORDER for x in ORDER for y in (1, 0)]
TREES = (("x", 1), ("z", 1), ("x", -1), ("z", -1))

SEND_US = 1.42
HOP_US = 4.5
LOAD_US = 4.0
GRAD_US = 0.42
GRAD_SLACK = 1.0
TILE_US = 0.55
TILE_SLACK = 0.6
BACKLOG = 3
ADD_US = 0.06
ISSUE_US = 0.05
REDUCE_FROM = 8.0
GATHER_FROM = 99.0
GATHER_TO = 99.0
NEAR = 1.0
MIX = 0.0
SEED = 0
DEPTH = 4


def tree_parent(tree, node):
    first, sign = tree
    x, y, z = node
    a, b = (x, z) if first == "x" else (z, x)
    second = "z" if first == "x" else "x"

    def back(v):
        if sign > 0:
            return {1: (0, "+"), 2: (1, "+"), 3: (0, "-")}[v]
        return {3: (0, "-"), 2: (3, "-"), 1: (0, "+")}[v]

    if b == 2 and y == 1 and a in (0, 2):
        a, y, b, link = a, 0, b, "y"
    elif b:
        b, way = back(b)
        link = second + way
    elif y:
        y, link = 0, "y"
    else:
        a, way = back(a)
        link = first + way
    return ((a, y, b) if first == "x" else (b, y, a)), link


def make_trees():
    parent, children = {}, {}
    for s, tree in enumerate(TREES):
        for node in NODES:
            children.setdefault((s, node), [])
        for node in NODES:
            if node != ROOT:
                up, link = tree_parent(tree, node)
                parent[s, node] = (up, link)
                children[s, up].append((node, link))
    return parent, children


PARENT, CHILDREN = make_trees()
EDGES = {key: i for i, key in enumerate(sorted(PARENT))}


def plan_links():
    def height(key):
        return 1 + max([height((key[0], c)) for c, _ in CHILDREN[key]], default=0)

    def depth(key):
        return 0 if key[1] == ROOT else 1 + depth((key[0], PARENT[key][0]))

    grad_at = {node: LOAD_US + GRAD_US * GRAD_SLACK * (i + 1) for i, node in enumerate(NODES)}
    waiting = {key: len(v) for key, v in CHILDREN.items()}
    latest = {key: grad_at[key[1]] for key in CHILDREN}
    ready = {link: [] for link in LINKS}
    free = {link: 0.0 for link in LINKS}
    for s in range(NSTREAM):
        for node, link in CHILDREN[s, ROOT]:
            ready[link].append((0.0, "gather", s, node))
    for key in PARENT:
        if not waiting[key]:
            ready[BACK[PARENT[key][1]]].append((latest[key], "reduce") + key)
    sends, arrival, roots, begun = [], {}, {}, {}
    while any(ready.values()):
        at, link = min((max(free[k], min(r[0] for r in v)), k) for k, v in ready.items() if v)
        open_now = [r for r in ready[link] if r[0] <= at + 1e-9]

        def rank(r):
            key = r[2:]
            mixed = MIX * ((EDGES[key] * 37 + SEED) % 101) / 101
            if r[1] == "reduce":
                first = REDUCE_FROM <= at and not GATHER_FROM <= at < GATHER_TO
                return (1 if first else -1, depth(key) + mixed, -r[0], -EDGES[key])
            return (0, height(key) + NEAR * begun.get(key[1], 0) + mixed, -r[0], -EDGES[key])

        pick = max(open_now, key=rank)
        ready[link].remove(pick)
        _, kind, s, node = pick
        free[link] = at + SEND_US
        there = at + SEND_US + HOP_US
        sends.append((at, link, kind, s, node))
        arrival[kind, s, node] = there
        if kind == "gather":
            begun[node] = begun.get(node, 0) + 1
            for child, way in CHILDREN[s, node]:
                ready[way].append((there, "gather", s, child))
        else:
            up = (s, PARENT[s, node][0])
            waiting[up] -= 1
            latest[up] = max(latest[up], there)
            if not waiting[up]:
                if up[1] == ROOT:
                    roots[s] = latest[up]
                else:
                    ready[BACK[PARENT[up][1]]].append((latest[up] + ADD_US, "reduce") + up)
    return sends, arrival, max(roots.values())


def make_program():
    sends, arrival, roots_at = plan_links()
    full_at = {n: max(arrival["gather", s, n] for s in range(NSTREAM)) for n in NODES if n != ROOT}
    full_at[ROOT] = 0.0
    tiles_left = sorted(NODES, key=lambda n: full_at[n])
    order = {node: i for i, node in enumerate(NODES)}
    tail = [(roots_at, "update"), (roots_at + 6.0, "outer"), (roots_at + 12.0, "spread")]
    events = sorted([(t, 1, ("send",) + tuple(r)) for t, *r in sends] + [(t, 0, (n,)) for t, n in tail], key=lambda e: e[:2])
    program, now, grads = [], 0.0, 0
    for at, _, op in events:
        need = order[op[3 + 1]] + 1 if op[0] == "send" and op[2] == "reduce" else 0
        while True:
            if grads < max(need, NSHARD * (op[0] != "send")):
                pass
            elif grads < NSHARD and max(now, LOAD_US) + 0.5 * GRAD_US < at:
                pass
            elif grads == NSHARD and tiles_left and full_at[tiles_left[0]] < now:
                backlog = sum(full_at[n] < now for n in tiles_left)
                if now + TILE_SLACK * TILE_US < at or backlog > BACKLOG:
                    program.append(("tile", tiles_left.pop(0)))
                    now += TILE_US
                    continue
                break
            else:
                break
            program.append(("grad", grads))
            now = max(now, LOAD_US) + GRAD_US
            grads += 1
        now = max(now, at) + (ADD_US if op[0] == "send" and op[2] == "reduce" else ISSUE_US)
        program.append(op)
    program += [("tile", n) for n in tiles_left]
    return program


def adam(weight, grad, first, second):
    first_next = beta_first * first + (1.0 - beta_first) * grad
    second_next = beta_second * second + (1.0 - beta_second) * grad * grad
    step = first_next / correction_first / (jnp.sqrt(second_next / correction_second) + adam_eps)
    return weight - adam_rate * (step + decay_rate * weight), first_next, second_next


def select_block(fragment, array):
    block = array[:, :FRAGW]
    for f in range(1, KW // FRAGW):
        block = jnp.where(fragment == f, array[:, f * FRAGW : (f + 1) * FRAGW], block)
    return block


def exchange_kernel(
    fragment_hbm, tokens_hbm, cot_hbm, weight_hbm, first_hbm, second_hbm, outer_hbm, mom_hbm,
    keys_ref, input_ref, inner_ref, first_ref, second_ref, outer_ref, mom_ref,
    fragment_ref, tokens, cot, weight, first, second, outer, mom, full, sums, landed, keys_acc, grad, inner, peers, spread,
    in_sem, send_sem, gather_sem, reduce_sem, peer_send, peer_recv, spread_send, spread_recv, ready,
):
    shard, rep = lax.axis_index("shard"), lax.axis_index("replica")
    my, mx, mz = shard % 2, (shard // 2) % 4, shard // 8
    core, high = rep % 2, rep // 2

    def owner(node):
        x, y, z = node
        return (((mz + 4 - z) % 4) * 4 + (mx + 4 - x) % 4) * 2 + (my + y) % 2

    def shard_at(link):
        x, y, z = mx, my, mz
        if link == "y":
            y = 1 - y
        elif link[0] == "x":
            x = (x + (1 if link[1] == "+" else 3)) % 4
        else:
            z = (z + (1 if link[1] == "+" else 3)) % 4
        return (z * 4 + x) * 2 + y

    there = {link: {"shard": shard_at(link)} for link in LINKS}
    peer = [high * 2 + 1 - core, (1 - high) * 2 + core, (1 - high) * 2 + 1 - core]

    def local(src, dst, i):
        return pltpu.make_async_copy(src, dst, in_sem.at[i])

    loads = [
        local(weight_hbm.at[0], weight, 0),
        local(cot_hbm, cot, 1),
        local(tokens_hbm, tokens, 2),
        local(first_hbm.at[0], first, 3),
        local(second_hbm.at[0], second, 4),
        local(outer_hbm, outer, 5),
        local(mom_hbm, mom, 6),
        local(fragment_hbm, fragment_ref, 7),
    ]
    loads[0].start()
    barrier = pltpu.get_barrier_semaphore()
    for link in LINKS:
        pl.semaphore_signal(barrier, inc=1, device_id=there[link], device_id_type=MESH)
    for p in peer:
        @pl.when(p > rep)
        def _():
            pl.semaphore_signal(barrier, inc=1, device_id={"replica": p}, device_id_type=MESH)

    loads[0].wait()
    for copy in loads[1:]:
        copy.start()
    full[shard] = weight[...].astype(BF16)
    pl.semaphore_wait(barrier, len(LINKS) + rep)
    for p in peer:
        @pl.when(p < rep)
        def _():
            pl.semaphore_signal(ready, inc=1, device_id={"replica": p}, device_id_type=MESH)


    def part(s):
        return pl.ds(s * PART, PART)

    issued = {link: [] for link in LINKS}
    waited = set()

    def send_copy(kind, s, node, slot):
        edge = EDGES[s, node]
        up, link = PARENT[s, node]
        if kind == "gather":
            where = full.at[owner(up), part(s)]
            return pltpu.make_async_remote_copy(
                src_ref=where, dst_ref=where, send_sem=send_sem.at[LINKS.index(link), slot],
                recv_sem=gather_sem.at[edge], device_id=there[link], device_id_type=MESH,
            )
        link = BACK[link]
        return pltpu.make_async_remote_copy(
            src_ref=sums.at[owner(node), part(s)], dst_ref=landed.at[edge],
            send_sem=send_sem.at[LINKS.index(link), slot],
            recv_sem=reduce_sem.at[edge], device_id=there[link], device_id_type=MESH,
        )

    def arrived(kind, s, node):
        if (kind, s, node) in waited or node == ROOT:
            return
        waited.add((kind, s, node))
        edge = EDGES[s, node]
        if kind == "gather":
            where = full.at[owner(node), part(s)]
            pltpu.make_async_copy(where, where, gather_sem.at[edge]).wait()
        else:
            where = landed.at[edge]
            pltpu.make_async_copy(where, where, reduce_sem.at[edge]).wait()

    def summed(s, node):
        total = sums[owner(node), part(s)].astype(F32)
        for child, _ in CHILDREN[s, node]:
            arrived("reduce", s, child)
            total = total + landed[EDGES[s, child]].astype(F32)
        return total

    def send(link, kind, s, node):
        if kind == "gather":
            arrived("gather", s, PARENT[s, node][0])
        elif CHILDREN[s, node]:
            sums[owner(node), part(s)] = summed(s, node).astype(BF16)
        line = issued[link]
        if len(line) >= DEPTH:
            line[-DEPTH].wait_send()
        copy = send_copy(kind, s, node, len(line) % DEPTH)
        copy.start()
        line.append(copy)

    def grad_tile(node):
        which = owner(node)
        cols = pl.ds(pl.multiple_of(which * ROWS, ROWS), ROWS)
        sums[which] = lax.dot_general(
            tokens[:, cols], cot[...], (((0,), (0,)), ((), ())), preferred_element_type=F32
        ).astype(BF16)

    def weight_tile(node, begin):
        for s in range(NSTREAM):
            arrived("gather", s, node)
        which = owner(node)
        cols = pl.ds(pl.multiple_of(which * ROWS, ROWS), ROWS)
        term = jnp.dot(tokens[:, cols], full[which], preferred_element_type=F32)
        if begin:
            keys_acc[...] = term
        else:
            keys_acc[...] += term
        back = lax.dot_general(cot[...], full[which], (((1,), (1,)), ((), ())), preferred_element_type=F32)
        input_ref[:, cols] = (back * SCALE).astype(BF16)

    mine = pl.ds(pl.multiple_of(rep * (ROWS // NREP), ROWS // NREP), ROWS // NREP)

    def update():
        for s in range(NSTREAM):
            grad[part(s), :] = summed(s, ROOT) * GRAD_SCALE
        for copy in loads[3:]:
            copy.wait()
        f = fragment_ref[0]
        inner[...] = adam(
            select_block(f, weight[...]), select_block(f, grad[...]),
            select_block(f, first[...]), select_block(f, second[...]),
        )[0]

        @pl.when(rep < NREP - 1)
        def _():
            pl.semaphore_wait(ready, NREP - 1 - rep)

        for copy in to_peers():
            copy.start()
        inner_ref[0], first_ref[0], second_ref[0] = adam(weight[...], grad[...], first[...], second[...])

    def to_peers():
        return [
            pltpu.make_async_remote_copy(
                src_ref=inner.at[pl.ds(pl.multiple_of(p * (ROWS // NREP), ROWS // NREP), ROWS // NREP)],
                dst_ref=peers.at[k], send_sem=peer_send.at[k], recv_sem=peer_recv.at[k],
                device_id={"replica": p}, device_id_type=MESH,
            )
            for k, p in enumerate(peer)
        ]

    def to_all():
        return [
            pltpu.make_async_remote_copy(
                src_ref=spread.at[mine], dst_ref=spread.at[mine], send_sem=spread_send.at[k],
                recv_sem=spread_recv.at[k], device_id={"replica": p}, device_id_type=MESH,
            )
            for k, p in enumerate(peer)
        ]

    def outer_step():
        total = inner[mine]
        for k, copy in enumerate(to_peers()):
            copy.wait_recv()
            total = total + peers[k]
        pseudo = outer[...] - total / NREP
        mom_next = outer_beta * mom[...] + pseudo
        outer_next = outer[...] - outer_rate * (pseudo + outer_beta * mom_next)
        outer_ref[...] = outer_next
        mom_ref[...] = mom_next
        spread[mine] = outer_next
        for copy in to_all():
            copy.start()

    def spread_step():
        for k, p in enumerate(peer):
            rows = pl.ds(pl.multiple_of(p * (ROWS // NREP), ROWS // NREP), ROWS // NREP)
            pltpu.make_async_copy(spread.at[rows], spread.at[rows], spread_recv.at[k]).wait()
        mixed = mixing_weight * inner[...] + (1.0 - mixing_weight) * spread[...]
        for f in range(KW // FRAGW):
            cols = slice(f * FRAGW, (f + 1) * FRAGW)
            inner_ref[0, :, cols] = jnp.where(fragment_ref[0] == f, mixed, inner_ref[0, :, cols])

    program = make_program()
    at, begin = 0, True
    while at < len(program):
        op = program[at]
        if op[0] == "grad":
            if op[1] == 0:
                loads[1].wait()
                loads[2].wait()
            grad_tile(NODES[op[1]])
        elif op[0] == "send":
            send(*op[1:])
        elif op[0] == "tile":
            weight_tile(op[1], begin)
            begin = False
        else:
            {"update": update, "outer": outer_step, "spread": spread_step}[op[0]]()
        at += 1

    keys_ref[...] = (keys_acc[...] * SCALE).astype(BF16)
    for line in issued.values():
        for copy in line[-DEPTH:]:
            copy.wait_send()
    for copy in to_peers() + to_all():
        copy.wait_send()


def finish_kernel(*refs):
    half = (len(refs) - 1) // 2
    sems = refs[-1]
    copies = []
    for src, dst in zip(refs[:half], refs[half:-1]):
        cuts = 4 if src.size > 2**20 else 1
        rows = src.shape[0] // cuts
        for c in range(cuts):
            where = pl.ds(c * rows, rows)
            copies.append(pltpu.make_async_copy(src.at[where], dst.at[where], sems.at[len(copies)]))
            copies[-1].start()
    for copy in copies:
        copy.wait()


OUTS = (
    ((TOK, KW), BF16),
    ((TOK, D), BF16),
    ((1, ROWS, KW), F32),
    ((1, ROWS, KW), F32),
    ((1, ROWS, KW), F32),
    ((ROWS // NREP, FRAGW), F32),
    ((ROWS // NREP, FRAGW), F32),
)


def exchange(fragment, tokens, cotangent, inner_weight, first_moment, second_moment, outer_params, outer_momentum):
    anyspace = pl.BlockSpec(memory_space=pl.ANY)
    vmem = pl.BlockSpec(memory_space=pltpu.VMEM)
    edges = len(EDGES)
    return pl.pallas_call(
        exchange_kernel,
        out_shape=[pltpu.VMEM(shape, dtype) for shape, dtype in OUTS],
        in_specs=[anyspace] * 8,
        out_specs=[vmem] * len(OUTS),
        scratch_shapes=[
            pltpu.SMEM((1,), jnp.int32),
            pltpu.VMEM((TOK, D), BF16),
            pltpu.VMEM((TOK, KW), BF16),
            pltpu.VMEM((ROWS, KW), F32),
            pltpu.VMEM((ROWS, KW), F32),
            pltpu.VMEM((ROWS, KW), F32),
            pltpu.VMEM((ROWS // NREP, FRAGW), F32),
            pltpu.VMEM((ROWS // NREP, FRAGW), F32),
            pltpu.VMEM((NSHARD, ROWS, KW), BF16),
            pltpu.VMEM((NSHARD, ROWS, KW), BF16),
            pltpu.VMEM((edges, PART, KW), BF16),
            pltpu.VMEM((TOK, KW), F32),
            pltpu.VMEM((ROWS, KW), F32),
            pltpu.VMEM((ROWS, FRAGW), F32),
            pltpu.VMEM((NREP - 1, ROWS // NREP, FRAGW), F32),
            pltpu.VMEM((ROWS, FRAGW), F32),
            pltpu.SemaphoreType.DMA((8,)),
            pltpu.SemaphoreType.DMA((len(LINKS), DEPTH)),
            pltpu.SemaphoreType.DMA((edges,)),
            pltpu.SemaphoreType.DMA((edges,)),
            pltpu.SemaphoreType.DMA((NREP - 1,)),
            pltpu.SemaphoreType.DMA((NREP - 1,)),
            pltpu.SemaphoreType.DMA((NREP - 1,)),
            pltpu.SemaphoreType.DMA((NREP - 1,)),
            pltpu.SemaphoreType.REGULAR,
        ],
        compiler_params=pltpu.CompilerParams(
            collective_id=0, has_side_effects=True, vmem_limit_bytes=46 * 2**20
        ),
        cost_estimate=pl.CostEstimate(
            flops=6 * TOK * D * KW, bytes_accessed=30 * 2**20, transcendentals=0
        ),
        name="exchange",
    )(fragment, tokens, cotangent, inner_weight, first_moment, second_moment, outer_params, outer_momentum)


def finish(*arrays):
    return pl.pallas_call(
        finish_kernel,
        out_shape=[pltpu.HBM(a.shape, a.dtype) for a in arrays],
        in_specs=[pl.BlockSpec(memory_space=pltpu.VMEM)] * len(arrays),
        out_specs=[pl.BlockSpec(memory_space=pltpu.HBM)] * len(arrays),
        scratch_shapes=[pltpu.SemaphoreType.DMA((16,))],
        compiler_params=pltpu.CompilerParams(vmem_limit_bytes=2 * 2**20),
        cost_estimate=pl.CostEstimate(flops=0, bytes_accessed=13 * 2**20, transcendentals=0),
        name="finish",
    )(*[pltpu.with_memory_space_constraint(a, pltpu.VMEM) for a in arrays])


def local_step(tokens, cotangent, inner_weight, first_moment, second_moment, outer_params, outer_momentum, fragment):
    outs = exchange(
        fragment, tokens, cotangent, inner_weight, first_moment, second_moment, outer_params, outer_momentum
    )
    return tuple(finish(*outs))


def solution(mesh):
    tokens = P(("replica", "shard"), None)
    state = P("replica", "shard", None)
    owned = P(("shard", "replica"), None)
    return jax.shard_map(
        local_step,
        mesh=mesh,
        in_specs=(tokens, tokens, state, state, state, owned, owned, P()),
        out_specs=(tokens, tokens, state, state, state, owned, owned),
        check_vma=False,
    )
```

```python
import functools

import jax
import jax.numpy as jnp
from jax import lax
from jax.experimental import pallas as pl
from jax.experimental.pallas import tpu as pltpu
from jax.sharding import PartitionSpec as P

MESH = pl.DeviceIdType.MESH
BF16 = jnp.bfloat16
F32 = jnp.float32

beta_first = 0.9
beta_second = 0.95
adam_rate = 0.05
decay_rate = 0.1
adam_eps = 1e-08
correction_first = 0.9999734386011124
correction_second = 0.994079470779666
outer_rate = 0.7
outer_beta = 0.9
mixing_weight = 0.5

D, KW, FRAGW, TOK, ROWS = 8192, 512, 128, 640, 256
NSHARD, NREP = 32, 4
SCALE = D ** (-0.5)
GRAD_SCALE = (TOK * NSHARD) ** (-0.5)
NSTREAM = 4
PART = ROWS // NSTREAM

LINKS = ("x+", "x-", "z+", "z-", "y")
BACK = {"x+": "x-", "x-": "x+", "z+": "z-", "z-": "z+", "y": "y"}
ROOT = (0, 0, 0)
ORDER = (2, 1, 3, 0)
NODES = [(x, y, z) for z in ORDER for x in ORDER for y in (1, 0)]
TREES = (("x", 1), ("z", 1), ("x", -1), ("z", -1))

SEND_US = 1.42
HOP_US = 4.5
LOAD_US = 4.0
GRAD_US = 0.42
GRAD_SLACK = 1.0
TILE_US = 0.55
TILE_SLACK = 0.6
BACKLOG = 3
ADD_US = 0.06
ISSUE_US = 0.05
REDUCE_FROM = 8.0
GATHER_FROM = 99.0
GATHER_TO = 99.0
NEAR = 1.0
MIX = 0.0
SEED = 0
DEPTH = 4


def tree_parent(tree, node):
    first, sign = tree
    x, y, z = node
    a, b = (x, z) if first == "x" else (z, x)
    second = "z" if first == "x" else "x"

    def back(v):
        if sign > 0:
            return {1: (0, "+"), 2: (1, "+"), 3: (0, "-")}[v]
        return {3: (0, "-"), 2: (3, "-"), 1: (0, "+")}[v]

    if b == 2 and y == 1 and a in (0, 2):
        a, y, b, link = a, 0, b, "y"
    elif b:
        b, way = back(b)
        link = second + way
    elif y:
        y, link = 0, "y"
    else:
        a, way = back(a)
        link = first + way
    return ((a, y, b) if first == "x" else (b, y, a)), link


def make_trees():
    parent, children = {}, {}
    for s, tree in enumerate(TREES):
        for node in NODES:
            children.setdefault((s, node), [])
        for node in NODES:
            if node != ROOT:
                up, link = tree_parent(tree, node)
                parent[s, node] = (up, link)
                children[s, up].append((node, link))
    return parent, children


PARENT, CHILDREN = make_trees()
EDGES = {key: i for i, key in enumerate(sorted(PARENT))}


def plan_links():
    def height(key):
        return 1 + max([height((key[0], c)) for c, _ in CHILDREN[key]], default=0)

    def depth(key):
        return 0 if key[1] == ROOT else 1 + depth((key[0], PARENT[key][0]))

    grad_at = {node: LOAD_US + GRAD_US * GRAD_SLACK * (i + 1) for i, node in enumerate(NODES)}
    waiting = {key: len(v) for key, v in CHILDREN.items()}
    latest = {key: grad_at[key[1]] for key in CHILDREN}
    ready = {link: [] for link in LINKS}
    free = {link: 0.0 for link in LINKS}
    for s in range(NSTREAM):
        for node, link in CHILDREN[s, ROOT]:
            ready[link].append((0.0, "gather", s, node))
    for key in PARENT:
        if not waiting[key]:
            ready[BACK[PARENT[key][1]]].append((latest[key], "reduce") + key)
    sends, arrival, roots, begun = [], {}, {}, {}
    while any(ready.values()):
        at, link = min((max(free[k], min(r[0] for r in v)), k) for k, v in ready.items() if v)
        open_now = [r for r in ready[link] if r[0] <= at + 1e-9]

        def rank(r):
            key = r[2:]
            mixed = MIX * ((EDGES[key] * 37 + SEED) % 101) / 101
            if r[1] == "reduce":
                first = REDUCE_FROM <= at and not GATHER_FROM <= at < GATHER_TO
                return (1 if first else -1, depth(key) + mixed, -r[0], -EDGES[key])
            return (0, height(key) + NEAR * begun.get(key[1], 0) + mixed, -r[0], -EDGES[key])

        pick = max(open_now, key=rank)
        ready[link].remove(pick)
        _, kind, s, node = pick
        free[link] = at + SEND_US
        there = at + SEND_US + HOP_US
        sends.append((at, link, kind, s, node))
        arrival[kind, s, node] = there
        if kind == "gather":
            begun[node] = begun.get(node, 0) + 1
            for child, way in CHILDREN[s, node]:
                ready[way].append((there, "gather", s, child))
        else:
            up = (s, PARENT[s, node][0])
            waiting[up] -= 1
            latest[up] = max(latest[up], there)
            if not waiting[up]:
                if up[1] == ROOT:
                    roots[s] = latest[up]
                else:
                    ready[BACK[PARENT[up][1]]].append((latest[up] + ADD_US, "reduce") + up)
    return sends, arrival, max(roots.values())


def make_program():
    sends, arrival, roots_at = plan_links()
    full_at = {n: max(arrival["gather", s, n] for s in range(NSTREAM)) for n in NODES if n != ROOT}
    full_at[ROOT] = 0.0
    tiles_left = sorted(NODES, key=lambda n: full_at[n])
    order = {node: i for i, node in enumerate(NODES)}
    tail = [(roots_at, "update"), (roots_at + 9.0, "outer"), (roots_at + 18.0, "spread")]
    events = sorted([(t, 1, ("send",) + tuple(r)) for t, *r in sends] + [(t, 0, (n,)) for t, n in tail], key=lambda e: e[:2])
    program, now, grads = [], 0.0, 0
    for at, _, op in events:
        need = order[op[3 + 1]] + 1 if op[0] == "send" and op[2] == "reduce" else 0
        while True:
            if grads < max(need, NSHARD * (op[0] != "send")):
                pass
            elif grads < NSHARD and max(now, LOAD_US) + 0.5 * GRAD_US < at:
                pass
            elif grads == NSHARD and tiles_left and full_at[tiles_left[0]] < now:
                backlog = sum(full_at[n] < now for n in tiles_left)
                if now + TILE_SLACK * TILE_US < at or backlog > BACKLOG:
                    program.append(("tile", tiles_left.pop(0)))
                    now += TILE_US
                    continue
                break
            else:
                break
            program.append(("grad", grads))
            now = max(now, LOAD_US) + GRAD_US
            grads += 1
        now = max(now, at) + (ADD_US if op[0] == "send" and op[2] == "reduce" else ISSUE_US)
        program.append(op)
    program += [("tile", n) for n in tiles_left]
    return program


def adam(weight, grad, first, second):
    first_next = beta_first * first + (1.0 - beta_first) * grad
    second_next = beta_second * second + (1.0 - beta_second) * grad * grad
    step = first_next / correction_first / (jnp.sqrt(second_next / correction_second) + adam_eps)
    return weight - adam_rate * (step + decay_rate * weight), first_next, second_next


def select_block(fragment, array):
    block = array[:, :FRAGW]
    for f in range(1, KW // FRAGW):
        block = jnp.where(fragment == f, array[:, f * FRAGW : (f + 1) * FRAGW], block)
    return block


def exchange_kernel(
    fragment_hbm, tokens_hbm, cot_hbm, weight_hbm, first_hbm, second_hbm, outer_hbm, mom_hbm,
    keys_ref, input_ref, inner_ref, first_ref, second_ref, outer_ref, mom_ref,
    fragment_ref, tokens, cot, weight, first, second, outer, mom, full, sums, landed, keys_acc, grad, inner, peers, spread,
    in_sem, send_sem, gather_sem, reduce_sem, peer_send, peer_recv, spread_send, spread_recv, ready,
):
    shard, rep = lax.axis_index("shard"), lax.axis_index("replica")
    my, mx, mz = shard % 2, (shard // 2) % 4, shard // 8
    core, high = rep % 2, rep // 2

    def owner(node):
        x, y, z = node
        return (((mz + 4 - z) % 4) * 4 + (mx + 4 - x) % 4) * 2 + (my + y) % 2

    def shard_at(link):
        x, y, z = mx, my, mz
        if link == "y":
            y = 1 - y
        elif link[0] == "x":
            x = (x + (1 if link[1] == "+" else 3)) % 4
        else:
            z = (z + (1 if link[1] == "+" else 3)) % 4
        return (z * 4 + x) * 2 + y

    there = {link: {"shard": shard_at(link)} for link in LINKS}
    peer = [high * 2 + 1 - core, (1 - high) * 2 + core, (1 - high) * 2 + 1 - core]

    def local(src, dst, i):
        return pltpu.make_async_copy(src, dst, in_sem.at[i])

    loads = [
        local(weight_hbm.at[0], weight, 0),
        local(cot_hbm, cot, 1),
        local(tokens_hbm, tokens, 2),
        local(first_hbm.at[0], first, 3),
        local(second_hbm.at[0], second, 4),
        local(outer_hbm, outer, 5),
        local(mom_hbm, mom, 6),
        local(fragment_hbm, fragment_ref, 7),
    ]
    loads[0].start()
    barrier = pltpu.get_barrier_semaphore()
    for link in LINKS:
        pl.semaphore_signal(barrier, inc=1, device_id=there[link], device_id_type=MESH)
    for p in peer:
        @pl.when(p > rep)
        def _():
            pl.semaphore_signal(barrier, inc=1, device_id={"replica": p}, device_id_type=MESH)

    loads[0].wait()
    for copy in loads[1:]:
        copy.start()
    full[shard] = weight[...].astype(BF16)
    pl.semaphore_wait(barrier, len(LINKS) + rep)
    for p in peer:
        @pl.when(p < rep)
        def _():
            pl.semaphore_signal(ready, inc=1, device_id={"replica": p}, device_id_type=MESH)


    def part(s):
        return pl.ds(s * PART, PART)

    issued = {link: [] for link in LINKS}
    waited = set()

    def send_copy(kind, s, node, slot):
        edge = EDGES[s, node]
        up, link = PARENT[s, node]
        if kind == "gather":
            where = full.at[owner(up), part(s)]
            return pltpu.make_async_remote_copy(
                src_ref=where, dst_ref=where, send_sem=send_sem.at[LINKS.index(link), slot],
                recv_sem=gather_sem.at[edge], device_id=there[link], device_id_type=MESH,
            )
        link = BACK[link]
        return pltpu.make_async_remote_copy(
            src_ref=sums.at[owner(node), part(s)], dst_ref=landed.at[edge],
            send_sem=send_sem.at[LINKS.index(link), slot],
            recv_sem=reduce_sem.at[edge], device_id=there[link], device_id_type=MESH,
        )

    def arrived(kind, s, node):
        if (kind, s, node) in waited or node == ROOT:
            return
        waited.add((kind, s, node))
        edge = EDGES[s, node]
        if kind == "gather":
            where = full.at[owner(node), part(s)]
            pltpu.make_async_copy(where, where, gather_sem.at[edge]).wait()
        else:
            where = landed.at[edge]
            pltpu.make_async_copy(where, where, reduce_sem.at[edge]).wait()

    def summed(s, node):
        total = sums[owner(node), part(s)].astype(F32)
        for child, _ in CHILDREN[s, node]:
            arrived("reduce", s, child)
            total = total + landed[EDGES[s, child]].astype(F32)
        return total

    def send(link, kind, s, node):
        if kind == "gather":
            arrived("gather", s, PARENT[s, node][0])
        elif CHILDREN[s, node]:
            sums[owner(node), part(s)] = summed(s, node).astype(BF16)
        line = issued[link]
        if len(line) >= DEPTH:
            line[-DEPTH].wait_send()
        copy = send_copy(kind, s, node, len(line) % DEPTH)
        copy.start()
        line.append(copy)

    def grad_tile(node):
        which = owner(node)
        cols = pl.ds(pl.multiple_of(which * ROWS, ROWS), ROWS)
        sums[which] = lax.dot_general(
            tokens[:, cols], cot[...], (((0,), (0,)), ((), ())), preferred_element_type=F32
        ).astype(BF16)

    def weight_tile(node, begin):
        for s in range(NSTREAM):
            arrived("gather", s, node)
        which = owner(node)
        cols = pl.ds(pl.multiple_of(which * ROWS, ROWS), ROWS)
        term = jnp.dot(tokens[:, cols], full[which], preferred_element_type=F32)
        if begin:
            keys_acc[...] = term
        else:
            keys_acc[...] += term
        back = lax.dot_general(cot[...], full[which], (((1,), (1,)), ((), ())), preferred_element_type=F32)
        input_ref[:, cols] = (back * SCALE).astype(BF16)

    mine = pl.ds(pl.multiple_of(rep * (ROWS // NREP), ROWS // NREP), ROWS // NREP)

    def update():
        for s in range(NSTREAM):
            grad[part(s), :] = summed(s, ROOT) * GRAD_SCALE
        for copy in loads[3:]:
            copy.wait()
        f = fragment_ref[0]
        inner[...] = adam(
            select_block(f, weight[...]), select_block(f, grad[...]),
            select_block(f, first[...]), select_block(f, second[...]),
        )[0]

        @pl.when(rep < NREP - 1)
        def _():
            pl.semaphore_wait(ready, NREP - 1 - rep)

        for copy in to_peers():
            copy.start()
        inner_ref[0], first_ref[0], second_ref[0] = adam(weight[...], grad[...], first[...], second[...])

    def to_peers():
        return [
            pltpu.make_async_remote_copy(
                src_ref=inner.at[pl.ds(pl.multiple_of(p * (ROWS // NREP), ROWS // NREP), ROWS // NREP)],
                dst_ref=peers.at[k], send_sem=peer_send.at[k], recv_sem=peer_recv.at[k],
                device_id={"replica": p}, device_id_type=MESH,
            )
            for k, p in enumerate(peer)
        ]

    def to_all():
        return [
            pltpu.make_async_remote_copy(
                src_ref=spread.at[mine], dst_ref=spread.at[mine], send_sem=spread_send.at[k],
                recv_sem=spread_recv.at[k], device_id={"replica": p}, device_id_type=MESH,
            )
            for k, p in enumerate(peer)
        ]

    def outer_step():
        total = inner[mine]
        for k, copy in enumerate(to_peers()):
            copy.wait_recv()
            total = total + peers[k]
        pseudo = outer[...] - total / NREP
        mom_next = outer_beta * mom[...] + pseudo
        outer_next = outer[...] - outer_rate * (pseudo + outer_beta * mom_next)
        outer_ref[...] = outer_next
        mom_ref[...] = mom_next
        spread[mine] = outer_next
        for copy in to_all():
            copy.start()

    def spread_step():
        for k, p in enumerate(peer):
            rows = pl.ds(pl.multiple_of(p * (ROWS // NREP), ROWS // NREP), ROWS // NREP)
            pltpu.make_async_copy(spread.at[rows], spread.at[rows], spread_recv.at[k]).wait()
        mixed = mixing_weight * inner[...] + (1.0 - mixing_weight) * spread[...]
        for f in range(KW // FRAGW):
            cols = slice(f * FRAGW, (f + 1) * FRAGW)
            inner_ref[0, :, cols] = jnp.where(fragment_ref[0] == f, mixed, inner_ref[0, :, cols])

    program = make_program()
    at, begin = 0, True
    while at < len(program):
        op = program[at]
        if op[0] == "grad":
            if op[1] == 0:
                loads[1].wait()
                loads[2].wait()
            grad_tile(NODES[op[1]])
        elif op[0] == "send":
            send(*op[1:])
        elif op[0] == "tile":
            weight_tile(op[1], begin)
            begin = False
        else:
            {"update": update, "outer": outer_step, "spread": spread_step}[op[0]]()
        at += 1

    keys_ref[...] = (keys_acc[...] * SCALE).astype(BF16)
    for line in issued.values():
        for copy in line[-DEPTH:]:
            copy.wait_send()
    for copy in to_peers() + to_all():
        copy.wait_send()


def finish_kernel(*refs):
    half = (len(refs) - 1) // 2
    sems = refs[-1]
    copies = []
    for src, dst in zip(refs[:half], refs[half:-1]):
        cuts = 4 if src.size > 2**20 else 1
        rows = src.shape[0] // cuts
        for c in range(cuts):
            where = pl.ds(c * rows, rows)
            copies.append(pltpu.make_async_copy(src.at[where], dst.at[where], sems.at[len(copies)]))
            copies[-1].start()
    for copy in copies:
        copy.wait()


OUTS = (
    ((TOK, KW), BF16),
    ((TOK, D), BF16),
    ((1, ROWS, KW), F32),
    ((1, ROWS, KW), F32),
    ((1, ROWS, KW), F32),
    ((ROWS // NREP, FRAGW), F32),
    ((ROWS // NREP, FRAGW), F32),
)


def exchange(fragment, tokens, cotangent, inner_weight, first_moment, second_moment, outer_params, outer_momentum):
    anyspace = pl.BlockSpec(memory_space=pl.ANY)
    vmem = pl.BlockSpec(memory_space=pltpu.VMEM)
    edges = len(EDGES)
    return pl.pallas_call(
        exchange_kernel,
        out_shape=[pltpu.VMEM(shape, dtype) for shape, dtype in OUTS],
        in_specs=[anyspace] * 8,
        out_specs=[vmem] * len(OUTS),
        scratch_shapes=[
            pltpu.SMEM((1,), jnp.int32),
            pltpu.VMEM((TOK, D), BF16),
            pltpu.VMEM((TOK, KW), BF16),
            pltpu.VMEM((ROWS, KW), F32),
            pltpu.VMEM((ROWS, KW), F32),
            pltpu.VMEM((ROWS, KW), F32),
            pltpu.VMEM((ROWS // NREP, FRAGW), F32),
            pltpu.VMEM((ROWS // NREP, FRAGW), F32),
            pltpu.VMEM((NSHARD, ROWS, KW), BF16),
            pltpu.VMEM((NSHARD, ROWS, KW), BF16),
            pltpu.VMEM((edges, PART, KW), BF16),
            pltpu.VMEM((TOK, KW), F32),
            pltpu.VMEM((ROWS, KW), F32),
            pltpu.VMEM((ROWS, FRAGW), F32),
            pltpu.VMEM((NREP - 1, ROWS // NREP, FRAGW), F32),
            pltpu.VMEM((ROWS, FRAGW), F32),
            pltpu.SemaphoreType.DMA((8,)),
            pltpu.SemaphoreType.DMA((len(LINKS), DEPTH)),
            pltpu.SemaphoreType.DMA((edges,)),
            pltpu.SemaphoreType.DMA((edges,)),
            pltpu.SemaphoreType.DMA((NREP - 1,)),
            pltpu.SemaphoreType.DMA((NREP - 1,)),
            pltpu.SemaphoreType.DMA((NREP - 1,)),
            pltpu.SemaphoreType.DMA((NREP - 1,)),
            pltpu.SemaphoreType.REGULAR,
        ],
        compiler_params=pltpu.CompilerParams(
            collective_id=0, has_side_effects=True, vmem_limit_bytes=46 * 2**20
        ),
        cost_estimate=pl.CostEstimate(
            flops=6 * TOK * D * KW, bytes_accessed=30 * 2**20, transcendentals=0
        ),
        name="exchange",
    )(fragment, tokens, cotangent, inner_weight, first_moment, second_moment, outer_params, outer_momentum)


def finish(*arrays):
    return pl.pallas_call(
        finish_kernel,
        out_shape=[pltpu.HBM(a.shape, a.dtype) for a in arrays],
        in_specs=[pl.BlockSpec(memory_space=pltpu.VMEM)] * len(arrays),
        out_specs=[pl.BlockSpec(memory_space=pltpu.HBM)] * len(arrays),
        scratch_shapes=[pltpu.SemaphoreType.DMA((16,))],
        compiler_params=pltpu.CompilerParams(vmem_limit_bytes=2 * 2**20),
        cost_estimate=pl.CostEstimate(flops=0, bytes_accessed=13 * 2**20, transcendentals=0),
        name="finish",
    )(*[pltpu.with_memory_space_constraint(a, pltpu.VMEM) for a in arrays])


def local_step(tokens, cotangent, inner_weight, first_moment, second_moment, outer_params, outer_momentum, fragment):
    outs = exchange(
        fragment, tokens, cotangent, inner_weight, first_moment, second_moment, outer_params, outer_momentum
    )
    return tuple(finish(*outs))


def solution(mesh):
    tokens = P(("replica", "shard"), None)
    state = P("replica", "shard", None)
    owned = P(("shard", "replica"), None)
    return jax.shard_map(
        local_step,
        mesh=mesh,
        in_specs=(tokens, tokens, state, state, state, owned, owned, P()),
        out_specs=(tokens, tokens, state, state, state, owned, owned),
        check_vma=False,
    )
```
